32 devices in a mesh: dp: 8 (over z, x), mp: 4 (over y, core).
Axes of the slice: x: 2, y: 2, z: 4, core: 2. Of those that a mesh axis runs over, the one named last changes fastest.
Arguments:
- hidden: bfloat16 [10240, 8192], P('dp', 'mp'), may hold values from -6 to 6
- rewards: float32 [64, 160], P('dp'), may hold values from -4 to 4
- lengths: int32 [64], P('dp'), may hold values from 1 to 160, as said below
- dest_shard: int32 [64], P('dp'), may hold values from 0 to 7, as said below
- source_owner: int32 [64], P('dp'), may hold values from 0 to 7, as said below
- pack_offset: int32 [64], P('dp'), may hold values from 0 to 639, as said below
- segment_ids: int32 [5120], P('dp'), may hold values from 0 to 7, as said below
- norm_gain: float32 [8192], replicated, may hold values from 0.5 to 1.5
- w_query: bfloat16 [8192, 4096], P(None, 'mp'), may hold values from -1 to 1
- w_key: bfloat16 [8192, 512], P(None, 'mp'), may hold values from -1 to 1
- w_value: bfloat16 [8192, 512], P(None, 'mp'), may hold values from -0.0625 to 0.0625
- value_head: float32 [8192], P('mp'), may hold values from -0.0625 to 0.0625
- folded_head: float32 [4096], P('mp'), may hold values from -0.09375 to 0.09375
Outputs:
- values: float32 [64, 160], P('dp')
- advantages: float32 [64, 160], P('dp')
The draws below stay inside these ranges and needn't reach their ends.
Inputs may be any that keep to these rules, and one draw needn't show every extreme that they name: `lengths`: rows of a slot past its rollout's length are unused. Every critic shard holds a rollout of 160 rows. Some owner's 8 rollouts all have 160 rows. `dest_shard`: owner o packs its 8 rollouts on the shards o, o + 1, ..., o + 7, modulo the number of shards, one on each. `source_owner`: shard s packs one rollout from each of the owners s, s - 1, ..., s - 7, modulo the number of shards, in some order, agreeing with dest_shard. `pack_offset`: A shard's packed rollouts lie back to back in the order of their index, each with the length that lengths gives it, and fill all 640 rows. `segment_ids`: each packed row names the index of the packed rollout that holds it, as pack_offset and lengths lay them out.
All inputs are finite; a program needn't handle non-finite values.
Results may differ from the reference program's by a relative error of at most 0.007.
Values may be sent and summed in bfloat16 or wider, within the bound.
No kernel may reach another device: no remote copies, remote signals or barrier semaphores. Data moves between devices by JAX's collectives and lax.ppermute only.
A program may use at most 192 MiB of HBM per device.

```python
import math
import jax
import jax.numpy as jnp
from jax import lax

D = 8192
HEADS = 32
KV_HEADS = 4
HD = 128
BATCH = 8
SLOT = 160
PACK = 640
ROLL = 64
ROWS = 10240
N_DP = 8


def packing_plan(key):
    base_key = jax.random.fold_in(key, 11)
    subkeys = jax.random.split(base_key, 5)
    shard_count = ROLL // BATCH
    short_rows = 3 * SLOT
    column_ids = jnp.arange(BATCH, dtype=jnp.int32)[None, :]
    shard_ids = jnp.arange(shard_count, dtype=jnp.int32)[:, None]
    ranking = jax.random.randint(subkeys[0], (shard_count, BATCH), 0, 1 << 20) * BATCH + column_ids
    packed_order = jnp.argsort(ranking, axis=1).astype(jnp.int32)
    inverse_order = jnp.argsort(packed_order, axis=1).astype(jnp.int32)
    cut_ids = jnp.arange(1, short_rows, dtype=jnp.int32)[None, :]
    candidates = jax.random.randint(subkeys[1], (shard_count, short_rows - 1), 0, 1 << 20) * short_rows + cut_ids
    candidates = jnp.where((cut_ids == SLOT) | (cut_ids == 2 * SLOT), 1 << 30, candidates)
    candidates = jnp.where((shard_ids == 0) & (cut_ids == SLOT - 1), -1, candidates)
    chosen = jnp.argsort(candidates, axis=1)[:, :BATCH - 4].astype(jnp.int32) + 1
    fixed_cuts = jnp.concatenate([jnp.full((shard_count, 1), SLOT, jnp.int32), jnp.full((shard_count, 1), 2 * SLOT, jnp.int32)], axis=1)
    cut_points = jnp.sort(jnp.concatenate([chosen, fixed_cuts], axis=1), axis=1)
    bounds = jnp.concatenate([jnp.zeros((shard_count, 1), jnp.int32), cut_points, jnp.full((shard_count, 1), short_rows, jnp.int32)], axis=1)
    short_sizes = bounds[:, 1:] - bounds[:, :-1]
    busy_owner = jax.random.randint(subkeys[4], (), 0, shard_count)
    busy_step = (shard_ids - busy_owner) % shard_count
    busy_column = jnp.take_along_axis(inverse_order, jnp.minimum(busy_step, BATCH - 1), axis=1)
    long_at = jax.random.randint(subkeys[2], (shard_count, 1), 0, BATCH)
    long_at = jnp.where(busy_step < BATCH, busy_column, long_at)
    short_index = jnp.clip(jnp.where(column_ids < long_at, column_ids, column_ids - 1), 0, BATCH - 2)
    packed_sizes = jnp.where(column_ids == long_at, SLOT, jnp.take_along_axis(short_sizes, short_index, axis=1)).astype(jnp.int32)
    offsets = (jnp.cumsum(packed_sizes, axis=1) - packed_sizes).astype(jnp.int32)
    source = (shard_ids - packed_order) % shard_count
    row_ids = jnp.arange(PACK, dtype=jnp.int32)[None, :, None]
    segments = jnp.sum((row_ids >= offsets[:, None, :]).astype(jnp.int32), axis=2) - 1
    owner_rank = jax.random.randint(subkeys[3], (shard_count, BATCH), 0, 1 << 20) * BATCH + column_ids
    owner_order = jnp.argsort(owner_rank, axis=1).astype(jnp.int32)
    destination = (shard_ids + owner_order) % shard_count
    position_in = inverse_order.reshape(-1)[destination * BATCH + owner_order]
    owner_lengths = packed_sizes.reshape(-1)[destination * BATCH + position_in]
    return (owner_lengths.reshape(-1).astype(jnp.int32), destination.reshape(-1).astype(jnp.int32), source.reshape(-1).astype(jnp.int32), offsets.reshape(-1), segments.reshape(-1).astype(jnp.int32))


def draw_lengths(key, part):
    return packing_plan(key)[0]


def draw_dest_shard(key, part):
    return packing_plan(key)[1]


def draw_source_owner(key, part):
    return packing_plan(key)[2]


def draw_pack_offset(key, part):
    return packing_plan(key)[3]


def draw_segment_ids(key, part):
    return packing_plan(key)[4]


def draw_w_key(key, part):
    own_key = jax.random.fold_in(key, 31)
    matrix = jnp.clip(jax.random.normal(own_key, (D, KV_HEADS * HD), jnp.float32), -6.0, 6.0) / math.sqrt(D)
    return jnp.clip(matrix, -1.0, 1.0).astype(jnp.bfloat16)


def draw_w_query(key, part):
    own_key = jax.random.fold_in(key, 37)
    matrix = jnp.clip(jax.random.normal(own_key, (D, HEADS * HD), jnp.float32), -6.0, 6.0) / math.sqrt(D)
    return jnp.clip(matrix, -1.0, 1.0).astype(jnp.bfloat16)


def block_levels(rng, dims, cuts, smallest, high):
    gain, own = 1.0, jax.random.fold_in(rng, 6)
    for position, shards_of in cuts:
        heights = jnp.exp(jax.random.uniform(jax.random.fold_in(own, position), (shards_of,), jnp.float32, smallest / len(cuts), high / len(cuts)))
        gain = gain * jnp.repeat(heights, dims[position] // shards_of).reshape([-1 if axis == position else 1 for axis in range(len(dims))])
    return gain


def centred(key, extent, width, most, pieces=(), held_as=jnp.bfloat16):
    drawn = width * jax.random.normal(key, extent, jnp.float32)
    if pieces:
        drawn = drawn * block_levels(key, extent, pieces, -0.22, 0.18)
    return jnp.clip(drawn, -most, most).astype(held_as)


def setup_inputs(seed: int = 0) -> dict:
    key_list = jax.random.split(jax.random.key(seed), 14)
    hidden = centred(key_list[0], (ROWS, D), 1.0, 6.0, ((0, 8), (1, 4)))
    rewards = centred(key_list[1], (ROLL, SLOT), 0.5, 4.0, ((0, 8),), jnp.float32)
    lengths = draw_lengths(jax.random.fold_in(key_list[13], 71), 0)
    dest_shard = draw_dest_shard(jax.random.fold_in(key_list[13], 71), 0)
    source_owner = draw_source_owner(jax.random.fold_in(key_list[13], 71), 0)
    pack_offset = draw_pack_offset(jax.random.fold_in(key_list[13], 71), 0)
    segment_ids = draw_segment_ids(jax.random.fold_in(key_list[13], 71), 0)
    norm_gain = jnp.clip(1.0 + 0.1 * jax.random.normal(key_list[7], (D,), jnp.float32), 0.5, 1.5)
    w_query = draw_w_query(jax.random.fold_in(key_list[13], 71), 0)
    w_key = draw_w_key(jax.random.fold_in(key_list[13], 71), 0)
    w_value = centred(key_list[10], (D, KV_HEADS * HD), D ** -0.5, 0.0625, ((1, 4),))
    value_head = centred(key_list[11], (D,), D ** -0.5, 0.0625, ((0, 4),), jnp.float32)
    folded_head = centred(key_list[12], (HEADS * HD,), (HEADS * HD) ** -0.5, 0.09375, ((0, 4),), jnp.float32)
    return {"hidden": hidden, "rewards": rewards, "lengths": lengths, "dest_shard": dest_shard, "source_owner": source_owner, "pack_offset": pack_offset, "segment_ids": segment_ids, "norm_gain": norm_gain, "w_query": w_query, "w_key": w_key, "w_value": w_value, "value_head": value_head, "folded_head": folded_head}


EPSILON = 1e-05
DISCOUNT = 0.99
SMOOTHING = 0.95
ROPE_BASE = 500000.0

def rotary(values_in, positions):
    half_width = values_in.shape[-1] // 2
    frequency = ROPE_BASE ** (-jnp.arange(half_width, dtype=jnp.float32) / half_width)
    angles = positions.astype(jnp.float32)[:, None] * frequency[None, :]
    cosine = jnp.cos(angles)[:, None, :]
    sine_part = jnp.sin(angles)[:, None, :]
    front_half = values_in[..., :half_width]
    back_half = values_in[..., half_width:]
    return jnp.concatenate([front_half * cosine - back_half * sine_part, back_half * cosine + front_half * sine_part], axis=-1)

def head_values(queries, keys_out, values_out, segments, positions, folded_head):
    row_count = queries.shape[0]
    kv_count = keys_out.shape[1] // HD
    group_size = queries.shape[1] // HD // kv_count
    query_rot = rotary(queries.reshape(row_count, kv_count * group_size, HD), positions).astype(jnp.bfloat16)
    query_rot = query_rot.reshape(row_count, kv_count, group_size, HD)
    key_rot = rotary(keys_out.reshape(row_count, kv_count, HD), positions).astype(jnp.bfloat16)
    value_rows = values_out.astype(jnp.bfloat16).reshape(row_count, kv_count, HD)
    scores = jnp.einsum('qhgd,khd->hgqk', query_rot.astype(jnp.float32), key_rot.astype(jnp.float32)) / math.sqrt(HD)
    allowed = (segments[:, None] == segments[None, :]) & (positions[:, None] >= positions[None, :])
    scores = jnp.where(allowed[None, None], scores, -1e+30)
    row_max = lax.optimization_barrier(jnp.max(scores, axis=-1, keepdims=True))
    exp_scores = jnp.where(allowed[None, None], jnp.exp(scores - row_max), 0.0)
    row_total = lax.optimization_barrier(jnp.sum(exp_scores, axis=-1, keepdims=True))
    weights = (exp_scores / row_total).astype(jnp.bfloat16)
    attended = jnp.einsum('hgqk,khd->qhgd', weights.astype(jnp.float32), value_rows.astype(jnp.float32))
    return lax.optimization_barrier(jnp.sum(attended.reshape(row_count, -1) * folded_head[None, :], axis=1))

def advantage_of(values, rewards, lengths):
    step_ids = jnp.arange(values.shape[1], dtype=jnp.int32)
    live_mask = step_ids[None, :] < lengths[:, None]
    next_live = step_ids[None, :] + 1 < lengths[:, None]
    following = jnp.concatenate([values[:, 1:], jnp.zeros((values.shape[0], 1), jnp.float32)], axis=1)
    one_step = jnp.where(live_mask, rewards + DISCOUNT * jnp.where(next_live, following, 0.0) - values, 0.0)
    lag_matrix = (step_ids[:, None] - step_ids[None, :]).astype(jnp.float32)
    decay_table = jnp.where(lag_matrix >= 0, jnp.exp(lag_matrix * math.log(DISCOUNT * SMOOTHING)), 0.0)
    return jnp.dot(one_step, decay_table, precision=lax.Precision.HIGHEST)

def reference(hidden, rewards, lengths, dest_shard, source_owner, pack_offset, segment_ids, norm_gain, w_query, w_key, w_value, value_head, folded_head):
    owner_dest = dest_shard.reshape(N_DP, BATCH)
    shard_owner = source_owner.reshape(N_DP, BATCH)
    shard_offset = pack_offset.reshape(N_DP, BATCH)
    shard_segment = segment_ids.reshape(N_DP, PACK)
    slot_lanes = jnp.arange(BATCH, dtype=jnp.int32)

    def one_shard(shard_id):
        owners = shard_owner[shard_id]
        offsets = shard_offset[shard_id]
        segments = shard_segment[shard_id]
        slot_of = lax.optimization_barrier(jnp.sum(jnp.where(owner_dest[owners] == shard_id, slot_lanes[None, :], 0), axis=1)).astype(jnp.int32)
        positions = jnp.arange(PACK, dtype=jnp.int32) - offsets[segments]
        source_rows = ((owners[segments] * BATCH + slot_of[segments]) * SLOT + positions).astype(jnp.int32)
        packed = hidden[source_rows]
        packed_f = packed.astype(jnp.float32)
        row_scale = lax.rsqrt(lax.optimization_barrier(jnp.mean(packed_f * packed_f, axis=1)) + EPSILON)
        normed = (packed_f * row_scale[:, None] * norm_gain[None, :]).astype(jnp.bfloat16)
        queries = jnp.dot(normed, w_query, preferred_element_type=jnp.float32)
        keys_out = jnp.dot(normed, w_key, preferred_element_type=jnp.float32)
        values_out = jnp.dot(normed, w_value, preferred_element_type=jnp.float32)
        attention_term = head_values(queries, keys_out, values_out, segments, positions, folded_head)
        return attention_term + lax.optimization_barrier(jnp.sum(packed_f * value_head[None, :], axis=1))
    packed_values = lax.map(one_shard, jnp.arange(N_DP, dtype=jnp.int32))
    owner_ids = jnp.arange(ROLL, dtype=jnp.int32) // BATCH
    j_of = lax.optimization_barrier(jnp.sum(jnp.where(shard_owner[dest_shard] == owner_ids[:, None], slot_lanes[None, :], 0), axis=1)).astype(jnp.int32)
    start_of = shard_offset[dest_shard, j_of]
    step_ids = jnp.arange(SLOT, dtype=jnp.int32)
    row_index = jnp.minimum(start_of[:, None] + step_ids[None, :], PACK - 1).astype(jnp.int32)
    gathered = packed_values[dest_shard[:, None], row_index]
    values = jnp.where(step_ids[None, :] < lengths[:, None], gathered, 0.0)
    return (values, advantage_of(values, rewards, lengths))
```

```python
import functools
import math

import jax
import jax.numpy as jnp
from jax import lax
from jax.experimental import pallas as pl
from jax.experimental.pallas import tpu as pltpu
from jax.sharding import PartitionSpec as P

HD = 128
EPSILON = 1e-05
DISCOUNT = 0.99
SMOOTHING = 0.95
ROPE_BASE = 500000.0
DEPTH = 1024


def swapped(value, axis, bit):
    length = lax.axis_size(axis)
    return lax.ppermute(value, axis, [(i, i ^ bit) for i in range(length)])


def lane_groups(value):
    total = value[:, :HD]
    for at in range(HD, value.shape[1], HD):
        total = total + value[:, at : at + HD]
    return total


def add_products(x, gain_ref, wq_ref, wk_ref, wv_ref, q_acc, kv_acc, ss_acc):
    xf = x.astype(jnp.float32)
    ss_acc[...] += lane_groups(xf * xf)
    scaled = (xf * gain_ref[...]).astype(jnp.bfloat16)
    q_acc[...] += jnp.dot(scaled, wq_ref[...], preferred_element_type=jnp.float32)
    kv_acc[:, :HD] += jnp.dot(scaled, wk_ref[...], preferred_element_type=jnp.float32)
    kv_acc[:, HD:] += jnp.dot(scaled, wv_ref[...], preferred_element_type=jnp.float32)


def first_kernel(
    part_ref, own_ref, near_ref, gain_ref, wq_ref, wk_ref, wv_ref, head_ref,
    q_ref, kv_ref, ss_ref, vt_ref,
):
    step = pl.program_id(0)
    half = pl.num_programs(0) // 2

    @pl.when(step == 0)
    def _():
        q_ref[...] = jnp.zeros_like(q_ref)
        kv_ref[...] = jnp.zeros_like(kv_ref)
        ss_ref[...] = jnp.zeros_like(ss_ref)
        vt_ref[...] = jnp.zeros_like(vt_ref)

    weights = (gain_ref, wq_ref, wk_ref, wv_ref)

    @pl.when(step < half)
    def _():
        vt_ref[...] += lane_groups(own_ref[...].astype(jnp.float32) * head_ref[...])
        add_products(own_ref[...], *weights, q_ref, kv_ref, ss_ref)

    @pl.when(step >= half)
    def _():
        add_products(near_ref[...], *weights, q_ref, kv_ref, ss_ref)


def second_kernel(
    slot, part_ref, x0_ref, x1_ref, gain_ref, wq_ref, wk_ref, wv_ref,
    q_ref, kv_ref, ss_ref, vt_ref, cos_ref, sin_ref, folded_ref,
    out_ref, q_acc, kv_acc, ss_acc,
):
    step = pl.program_id(0)
    steps = pl.num_programs(0)
    rows = q_acc.shape[0]
    heads = q_acc.shape[1] // HD

    @pl.when(step == 0)
    def _():
        q_acc[...] = q_ref[...]
        kv_acc[...] = kv_ref[...]
        ss_acc[...] = ss_ref[...]

    weights = (gain_ref, wq_ref, wk_ref, wv_ref)

    @pl.when(step < steps // 2)
    def _():
        add_products(x0_ref[...], *weights, q_acc, kv_acc, ss_acc)

    @pl.when(step >= steps // 2)
    def _():
        add_products(x1_ref[...], *weights, q_acc, kv_acc, ss_acc)

    @pl.when(step == steps - 1)
    def _():
        features = DEPTH * steps * 2
        cosine, sine = cos_ref[...], sin_ref[...]
        row_at = lax.broadcasted_iota(jnp.int32, (slot, slot), 0)
        key_at = lax.broadcasted_iota(jnp.int32, (slot, slot), 1)
        allowed = row_at >= key_at
        ones = jnp.ones((8, HD), jnp.float32)

        def turned(value):
            return (value * cosine + pltpu.roll(value, HD // 2, 1) * sine).astype(jnp.bfloat16)

        def one_rollout(r, carry):
            here = pl.ds(pl.multiple_of(r * slot, 16), slot)
            mean = jnp.sum(ss_acc[here, :], axis=1, keepdims=True) / features
            scale = lax.rsqrt(mean + EPSILON)
            key = turned(kv_acc[here, :HD] * scale)
            val = (kv_acc[here, HD:] * scale).astype(jnp.bfloat16)
            total = vt_ref[here, :]
            for h in range(heads):
                query = turned(q_acc[here, h * HD : (h + 1) * HD] * scale)
                scores = lax.dot_general(
                    query, key, (((1,), (1,)), ((), ())), preferred_element_type=jnp.float32
                ) * (1.0 / math.sqrt(HD))
                scores = jnp.where(allowed, scores, -1e30)
                exps = jnp.exp(scores - jnp.max(scores, axis=1, keepdims=True))
                probs = (exps / jnp.sum(exps, axis=1, keepdims=True)).astype(jnp.bfloat16)
                attended = jnp.dot(probs, val, preferred_element_type=jnp.float32)
                total = total + attended * folded_ref[h : h + 1, :]
            out_ref[r] = lax.dot_general(
                ones, total, (((1,), (1,)), ((), ())),
                precision=lax.Precision.HIGHEST, preferred_element_type=jnp.float32,
            )
            return carry

        lax.fori_loop(0, rows // slot, one_rollout, 0)


def weight_specs(first, second, blocks, widths):
    def row(step, part_ref):
        flip = jnp.where(step < blocks, first, second)
        return (part_ref[0] ^ flip) * blocks + step % blocks

    return [pl.BlockSpec((1, DEPTH), lambda k, p: (0, row(k, p)))] + [
        pl.BlockSpec((DEPTH, width), lambda k, p: (row(k, p), 0)) for width in widths
    ]


def x_specs(rows, blocks):
    return [
        pl.BlockSpec((rows, DEPTH), lambda k, p: (0, jnp.minimum(k, blocks - 1))),
        pl.BlockSpec((rows, DEPTH), lambda k, p: (0, jnp.maximum(k - blocks, 0))),
    ]


def cost(rows, depth, columns):
    return pl.CostEstimate(
        flops=2 * rows * depth * columns,
        bytes_accessed=2 * depth * (rows + columns) + 4 * rows * columns,
        transcendentals=0,
    )


def local(
    hidden,
    rewards,
    lengths,
    dest_shard,
    source_owner,
    pack_offset,
    segment_ids,
    norm_gain,
    w_query,
    w_key,
    w_value,
    value_head,
    folded_head,
):
    rollouts, slot = rewards.shape
    rows, part_width = hidden.shape
    blocks = part_width // DEPTH
    q_width, kv_width = w_query.shape[1], w_key.shape[1]
    widths = (q_width, kv_width, kv_width)
    columns = sum(widths)
    part = lax.axis_index("mp").astype(jnp.int32)[None]
    gain = norm_gain[None, :]
    weights = (w_query, w_key, w_value)

    positions = jnp.arange(slot, dtype=jnp.float32)
    half = HD // 2
    frequency = ROPE_BASE ** (-jnp.arange(half, dtype=jnp.float32) / half)
    angles = positions[:, None] * frequency[None, :]
    cosine = jnp.concatenate([jnp.cos(angles)] * 2, axis=1)
    sine = jnp.concatenate([-jnp.sin(angles), jnp.sin(angles)], axis=1)

    near = swapped(hidden, "mp", 1)
    sums = pl.pallas_call(
        first_kernel,
        grid_spec=pltpu.PrefetchScalarGridSpec(
            num_scalar_prefetch=1,
            grid=(2 * blocks,),
            in_specs=x_specs(rows, blocks)
            + weight_specs(0, 1, blocks, widths)
            + [pl.BlockSpec((1, DEPTH), lambda k, p: (0, jnp.minimum(k, blocks - 1)))],
            out_specs=[
                pl.BlockSpec((rows, width), lambda k, p: (0, 0))
                for width in (q_width, 2 * kv_width, HD, HD)
            ],
        ),
        out_shape=[
            jax.ShapeDtypeStruct((rows, width), jnp.float32)
            for width in (q_width, 2 * kv_width, HD, HD)
        ],
        compiler_params=pltpu.CompilerParams(vmem_limit_bytes=56 << 20),
        cost_estimate=cost(rows, 2 * part_width, columns),
        name="own_half",
    )(part, hidden, near, gain, *weights, value_head[None, :])

    def far_half(begin, count, far, far_near):
        at = begin // count
        return pl.pallas_call(
            functools.partial(second_kernel, slot),
            grid_spec=pltpu.PrefetchScalarGridSpec(
                num_scalar_prefetch=1,
                grid=(2 * blocks,),
                in_specs=x_specs(count, blocks)
                + weight_specs(2, 3, blocks, widths)
                + [
                    pl.BlockSpec((count, width), lambda k, p: (at, 0))
                    for width in (q_width, 2 * kv_width, HD, HD)
                ]
                + [pl.BlockSpec((slot, HD), lambda k, p: (0, 0))] * 2
                + [pl.BlockSpec((q_width // HD, HD), lambda k, p: (0, 0))],
                out_specs=pl.BlockSpec((count // slot, 8, slot), lambda k, p: (0, 0, 0)),
                scratch_shapes=[
                    pltpu.VMEM((count, q_width), jnp.float32),
                    pltpu.VMEM((count, 2 * kv_width), jnp.float32),
                    pltpu.VMEM((count, HD), jnp.float32),
                ],
            ),
            out_shape=jax.ShapeDtypeStruct((count // slot, 8, slot), jnp.float32),
            compiler_params=pltpu.CompilerParams(vmem_limit_bytes=56 << 20),
            cost_estimate=cost(count, 2 * part_width, columns),
            name="far_half",
        )(
            part, far, far_near, gain, *weights, *sums, cosine, sine,
            folded_head.reshape(q_width // HD, HD),
        )[:, 0, :]

    terms = []
    begin = 0
    after = sums[3]
    for count in (3, 3, 1, 1):
        size = count * slot
        far = swapped(hidden[begin : begin + size], "mp", 2)
        far, after = lax.optimization_barrier((far, after))
        far_near = swapped(far, "mp", 1)
        terms.append(far_half(begin, size, far, far_near))
        after = terms[-1]
        begin += size
    slot_values = lax.psum(jnp.concatenate(terms, axis=0), "mp")

    step_ids = jnp.arange(slot, dtype=jnp.int32)
    live_mask = step_ids[None, :] < lengths[:, None]
    values = jnp.where(live_mask, slot_values, 0.0)
    next_live = step_ids[None, :] + 1 < lengths[:, None]
    following = jnp.concatenate([values[:, 1:], jnp.zeros((rollouts, 1), jnp.float32)], axis=1)
    one_step = jnp.where(
        live_mask, rewards + DISCOUNT * jnp.where(next_live, following, 0.0) - values, 0.0
    )
    lag_matrix = (step_ids[:, None] - step_ids[None, :]).astype(jnp.float32)
    decay_table = jnp.where(
        lag_matrix >= 0, jnp.exp(lag_matrix * math.log(DISCOUNT * SMOOTHING)), 0.0
    )
    advantages = jnp.dot(one_step, decay_table, precision=lax.Precision.HIGHEST)
    return (values, advantages)


def solution(mesh):
    return jax.shard_map(
        local,
        mesh=mesh,
        in_specs=(
            P("dp", "mp"),
            P("dp", None),
            P("dp"),
            P("dp"),
            P("dp"),
            P("dp"),
            P("dp"),
            P(),
            P(None, "mp"),
            P(None, "mp"),
            P(None, "mp"),
            P("mp"),
            P("mp"),
        ),
        out_specs=(P("dp", None), P("dp", None)),
        check_vma=False,
    )
```

```python
import functools
import math

import jax
import jax.numpy as jnp
from jax import lax
from jax.experimental import pallas as pl
from jax.experimental.pallas import tpu as pltpu
from jax.sharding import PartitionSpec as P

HD = 128
EPSILON = 1e-05
DISCOUNT = 0.99
SMOOTHING = 0.95
ROPE_BASE = 500000.0
DEPTH = 1024
GRAIN = 16
ROUTES = (1, 2, 4)
SLOT_AT, ARRIVED_AT, SHIP_SLOT, SHIPPED, OVERFLOW = 0, 16, 24, 32, 40


def swapped(value, axis, bit):
    length = lax.axis_size(axis)
    return lax.ppermute(value, axis, [(i, i ^ bit) for i in range(length)])


def lane_groups(value):
    total = value[:, :HD]
    for at in range(HD, value.shape[1], HD):
        total = total + value[:, at : at + HD]
    return total


def add_products(x, gain_ref, wq_ref, wk_ref, wv_ref, q_acc, kv_acc, ss_acc):
    xf = x.astype(jnp.float32)
    ss_acc[...] += lane_groups(xf * xf)
    scaled = (xf * gain_ref[...]).astype(jnp.bfloat16)
    q_acc[...] += jnp.dot(scaled, wq_ref[...], preferred_element_type=jnp.float32)
    kv_acc[:, :HD] += jnp.dot(scaled, wk_ref[...], preferred_element_type=jnp.float32)
    kv_acc[:, HD:] += jnp.dot(scaled, wv_ref[...], preferred_element_type=jnp.float32)


def first_kernel(
    part_ref, own_ref, near_ref, gain_ref, wq_ref, wk_ref, wv_ref, head_ref,
    q_ref, kv_ref, ss_ref, vt_ref,
):
    step = pl.program_id(0)
    half = pl.num_programs(0) // 2

    @pl.when(step == 0)
    def _():
        q_ref[...] = jnp.zeros_like(q_ref)
        kv_ref[...] = jnp.zeros_like(kv_ref)
        ss_ref[...] = jnp.zeros_like(ss_ref)
        vt_ref[...] = jnp.zeros_like(vt_ref)

    weights = (gain_ref, wq_ref, wk_ref, wv_ref)

    @pl.when(step < half)
    def _():
        vt_ref[...] += lane_groups(own_ref[...].astype(jnp.float32) * head_ref[...])
        add_products(own_ref[...], *weights, q_ref, kv_ref, ss_ref)

    @pl.when(step >= half)
    def _():
        add_products(near_ref[...], *weights, q_ref, kv_ref, ss_ref)


def turned(value, cosine, sine):
    return (value * cosine + pltpu.roll(value, HD // 2, 1) * sine).astype(jnp.bfloat16)


def second_kernel(
    slot, tile, begin, part_ref, place_ref, x0_ref, x1_ref, gain_ref, wq_ref, wk_ref, wv_ref,
    q_ref, kv_ref, ss_ref, vt_ref, cos_ref, sin_ref, folded_ref, key_in, val_in,
    out_ref, key_out, val_out, q_acc, kv_acc, ss_acc, cos_rows, sin_rows, place_rows, keys, vals,
):
    step = pl.program_id(0)
    steps = pl.num_programs(0)
    rows = q_acc.shape[0]
    heads = q_acc.shape[1] // HD

    @pl.when(step == 0)
    def _():
        q_acc[...] = q_ref[...]
        kv_acc[...] = kv_ref[...]
        ss_acc[...] = ss_ref[...]
        keys[:slot, :] = key_in[...]
        vals[:slot, :] = val_in[...]
        inner = lax.broadcasted_iota(jnp.int32, (GRAIN, HD), 0)

        def place(b, carry):
            at = place_ref[begin // GRAIN + b]
            here = pl.ds(pl.multiple_of(b * GRAIN, GRAIN), GRAIN)
            there = pl.ds(pl.multiple_of(at * GRAIN, GRAIN), GRAIN)
            cos_rows[here, :] = cos_ref[there, :]
            sin_rows[here, :] = sin_ref[there, :]
            place_rows[here, :] = inner + at * GRAIN
            return carry

        lax.fori_loop(0, rows // GRAIN, place, 0)

    weights = (gain_ref, wq_ref, wk_ref, wv_ref)

    @pl.when(step < steps // 2)
    def _():
        add_products(x0_ref[...], *weights, q_acc, kv_acc, ss_acc)

    @pl.when(step >= steps // 2)
    def _():
        add_products(x1_ref[...], *weights, q_acc, kv_acc, ss_acc)

    @pl.when(step == steps - 1)
    def _():
        features = DEPTH * steps * 2
        scale = lax.rsqrt(jnp.sum(ss_acc[...], axis=1, keepdims=True) / features + EPSILON)
        keys[slot:, :] = turned(kv_acc[:, :HD] * scale, cos_rows[...], sin_rows[...])
        vals[slot:, :] = (kv_acc[:, HD:] * scale).astype(jnp.bfloat16)
        key_out[...] = keys[rows:, :]
        val_out[...] = vals[rows:, :]
        back = (
            lax.broadcasted_iota(jnp.int32, (tile, slot + tile), 0)
            + slot
            - lax.broadcasted_iota(jnp.int32, (tile, slot + tile), 1)
        )

        def one_tile(t, carry):
            here = pl.ds(pl.multiple_of(t * tile, GRAIN), tile)
            window = pl.ds(pl.multiple_of(t * tile, GRAIN), slot + tile)
            mean = jnp.sum(ss_acc[here, :], axis=1, keepdims=True) / features
            scale = lax.rsqrt(mean + EPSILON)
            cosine, sine = cos_rows[here, :] * scale, sin_rows[here, :] * scale
            allowed = (back >= 0) & (back <= place_rows[here, :1])
            key, val = keys[window, :], vals[window, :]
            total = vt_ref[here, :]
            for h in range(heads):
                query = turned(q_acc[here, h * HD : (h + 1) * HD], cosine, sine)
                scores = lax.dot_general(
                    query, key, (((1,), (1,)), ((), ())), preferred_element_type=jnp.float32
                ) * (1.0 / math.sqrt(HD))
                scores = jnp.where(allowed, scores, -1e30)
                exps = jnp.exp(scores - jnp.max(scores, axis=1, keepdims=True))
                probs = (exps / jnp.sum(exps, axis=1, keepdims=True)).astype(jnp.bfloat16)
                attended = jnp.dot(probs, val, preferred_element_type=jnp.float32)
                total = total + attended * folded_ref[h : h + 1, :]
            out_ref[here, :] = total
            return carry

        lax.fori_loop(0, rows // tile, one_tile, 0)


def start_copy(source, source_block, target, target_block, sem):
    pltpu.make_async_copy(
        source.at[pl.ds(pl.multiple_of(source_block * GRAIN, GRAIN), GRAIN)],
        target.at[pl.ds(pl.multiple_of(target_block * GRAIN, GRAIN), GRAIN)],
        sem,
    ).start()


def wait_copies(source, target, sems, count):
    def wait(b, carry):
        pltpu.make_async_copy(
            source.at[pl.ds(0, GRAIN)],
            target.at[pl.ds(pl.multiple_of(b * GRAIN, GRAIN), GRAIN)],
            sems.at[b],
        ).wait()
        return carry

    lax.fori_loop(0, count, wait, 0)


def blocks_of(length):
    return (length + (GRAIN - 1)) >> (GRAIN.bit_length() - 1)


def lay_out(begin, count, slot_blocks, first_block, source_ref, place_ref):
    def enter(j, carry):
        source_ref[begin + j] = first_block + j
        place_ref[begin + j] = j
        return carry

    lax.fori_loop(0, count, enter, 0)


def lay_out_fill(slot_blocks, source_ref, place_ref):
    def enter(b, carry):
        source_ref[b] = b
        place_ref[b] = lax.rem(b, slot_blocks)
        return carry

    lax.fori_loop(0, source_ref.shape[0], enter, 0)


def first_pack_kernel(slot_blocks, lengths_ref, hidden_ref, out_ref, place_ref, source_ref, sems):
    lay_out_fill(slot_blocks, source_ref, place_ref)
    at = jnp.int32(0)
    for i in range(lengths_ref.shape[0]):
        count = blocks_of(lengths_ref[i])
        lay_out(at, count, slot_blocks, i * slot_blocks, source_ref, place_ref)
        at = at + count
    total = out_ref.shape[0] // GRAIN

    def start(b, carry):
        start_copy(hidden_ref, source_ref[b], out_ref, b, sems.at[b])
        return carry

    lax.fori_loop(0, total, start, 0)
    wait_copies(hidden_ref, out_ref, sems, total)


def plan_kernel(
    slot_blocks, first_blocks, capacity, me_ref, lengths_ref, hidden_ref,
    source_ref, place_ref, info_ref, *refs,
):
    ships, (kept, load, sent, moved, sems) = refs[: len(ROUTES)], refs[len(ROUTES) :]
    me = me_ref[0]
    owners = kept.shape[0]
    rollouts = lengths_ref.shape[0] // owners

    def begin(o, carry):
        total = jnp.int32(0)
        for i in range(rollouts):
            total = total + blocks_of(lengths_ref[o * rollouts + i])
        kept[o] = total
        load[o] = jnp.maximum(total, first_blocks)
        sent[o] = 0
        return carry

    lax.fori_loop(0, owners, begin, 0)
    arrived = []
    for r, bit in enumerate(ROUTES):

        def choose(o, carry):
            size = blocks_of(lengths_ref[o * rollouts + rollouts - 1 - sent[o]])
            useful = (kept[o] - size >= first_blocks) & (load[o ^ bit] + size < load[o])
            moved[o] = jnp.where(useful, size, 0)
            return carry

        lax.fori_loop(0, owners, choose, 0)
        slot_now = rollouts - 1 - sent[me]
        info_ref[SHIP_SLOT + r] = slot_now
        info_ref[SHIPPED + r] = jnp.where(moved[me] > 0, 1, 0)
        arrived.append(moved[me ^ bit])
        size = slot_blocks * GRAIN
        pltpu.make_async_copy(
            hidden_ref.at[pl.ds(pl.multiple_of(slot_now * size, GRAIN), size)],
            ships[r],
            sems.at[r],
        ).start()

        def move(o, carry):
            kept[o] = kept[o] - moved[o]
            load[o] = load[o] - moved[o] + moved[o ^ bit]
            sent[o] = sent[o] + jnp.where(moved[o] > 0, 1, 0)
            return carry

        lax.fori_loop(0, owners, move, 0)

    most = lax.fori_loop(0, owners, lambda o, m: jnp.maximum(m, load[o]), jnp.int32(0))
    info_ref[OVERFLOW] = jnp.where(most > capacity, 1, 0)

    lay_out_fill(slot_blocks, source_ref, place_ref)
    at = jnp.int32(0)
    for i in range(rollouts):
        here = i < rollouts - sent[me]
        count = jnp.where(here, blocks_of(lengths_ref[me * rollouts + i]), 0)
        info_ref[SLOT_AT + i] = jnp.where(here, at, 0)
        lay_out(at, count, slot_blocks, i * slot_blocks, source_ref, place_ref)
        at = at + count
    at = jnp.maximum(at, first_blocks)
    for r in range(len(ROUTES)):
        info_ref[ARRIVED_AT + r] = jnp.where(arrived[r] > 0, at, 0)
        lay_out(at, arrived[r], slot_blocks, (rollouts + r) * slot_blocks, source_ref, place_ref)
        at = at + arrived[r]
    for r in range(len(ROUTES)):
        pltpu.make_async_copy(hidden_ref.at[pl.ds(0, slot_blocks * GRAIN)], ships[r], sems.at[r]).wait()


def pack_kernel(begin, slot_blocks, source_ref, hidden_ref, *refs):
    arrivals, (out_ref, sems) = refs[: len(ROUTES)], refs[len(ROUTES) :]
    total = out_ref.shape[0] // GRAIN
    own = hidden_ref.shape[0] // GRAIN

    def start(b, carry):
        block = source_ref[begin // GRAIN + b]

        @pl.when(block < own)
        def _():
            start_copy(hidden_ref, block, out_ref, b, sems.at[b])

        for r, arrival in enumerate(arrivals):
            low = own + r * slot_blocks

            @pl.when((block >= low) & (block < low + slot_blocks))
            def _():
                start_copy(arrival, block - low, out_ref, b, sems.at[b])

        return carry

    lax.fori_loop(0, total, start, 0)
    wait_copies(hidden_ref, out_ref, sems, total)


def unpack_kernel(slot, rollouts, info_ref, *refs):
    totals, (out_ref, rows_ref) = refs[:-2], refs[-2:]
    at = 0
    for total in totals:
        rows_ref[at : at + total.shape[0], :] = total[...]
        at += total.shape[0]
    rows_ref[at:, :] = jnp.zeros((rows_ref.shape[0] - at, HD), jnp.float32)
    ones = jnp.ones((8, HD), jnp.float32)
    for i in range(out_ref.shape[0]):
        block = info_ref[SLOT_AT + i] if i < rollouts else info_ref[ARRIVED_AT + i - rollouts]
        part = rows_ref[pl.ds(pl.multiple_of(block * GRAIN, GRAIN), slot), :]
        sums = lax.dot_general(
            ones, part, (((1,), (1,)), ((), ())),
            precision=lax.Precision.HIGHEST, preferred_element_type=jnp.float32,
        )
        out_ref[i : i + 1, :] = sums[:1, :]


def weight_specs(first, second, blocks, widths):
    def row(step, part_ref, *rest):
        flip = jnp.where(step < blocks, first, second)
        return (part_ref[0] ^ flip) * blocks + step % blocks

    return [pl.BlockSpec((1, DEPTH), lambda k, *p: (0, row(k, *p)))] + [
        pl.BlockSpec((DEPTH, width), lambda k, *p: (row(k, *p), 0)) for width in widths
    ]


def x_specs(rows, blocks):
    return [
        pl.BlockSpec((rows, DEPTH), lambda k, *p: (0, jnp.minimum(k, blocks - 1))),
        pl.BlockSpec((rows, DEPTH), lambda k, *p: (0, jnp.maximum(k - blocks, 0))),
    ]


def cost(rows, depth, columns):
    return pl.CostEstimate(
        flops=2 * rows * depth * columns,
        bytes_accessed=2 * depth * (rows + columns) + 4 * rows * columns,
        transcendentals=0,
    )


def local(
    hidden,
    rewards,
    lengths,
    dest_shard,
    source_owner,
    pack_offset,
    segment_ids,
    norm_gain,
    w_query,
    w_key,
    w_value,
    value_head,
    folded_head,
):
    rollouts, slot = rewards.shape
    rows, part_width = hidden.shape
    blocks = part_width // DEPTH
    q_width, kv_width = w_query.shape[1], w_key.shape[1]
    widths = (q_width, kv_width, kv_width)
    columns = sum(widths)
    part = lax.axis_index("mp").astype(jnp.int32)[None]
    gain = norm_gain[None, :]
    weights = (w_query, w_key, w_value)

    positions = jnp.arange(slot, dtype=jnp.float32)
    half = HD // 2
    frequency = ROPE_BASE ** (-jnp.arange(half, dtype=jnp.float32) / half)
    angles = positions[:, None] * frequency[None, :]
    cosine = jnp.concatenate([jnp.cos(angles)] * 2, axis=1)
    sine = jnp.concatenate([-jnp.sin(angles), jnp.sin(angles)], axis=1)

    slot_blocks = slot // GRAIN
    packed = segment_ids.shape[0]
    first = packed * 3 // 4
    second = packed * 3 // 5
    rest = rows - first - second
    whole = jax.ShapeDtypeStruct
    anywhere = pl.BlockSpec(memory_space=pl.ANY)
    scalars = pl.BlockSpec(memory_space=pltpu.SMEM)
    onchip = pl.BlockSpec(memory_space=pltpu.VMEM)
    blocks_in_all = rows // GRAIN

    def own_half(x):
        count = x.shape[0]
        near = swapped(x, "mp", 1)
        return pl.pallas_call(
            first_kernel,
            grid_spec=pltpu.PrefetchScalarGridSpec(
                num_scalar_prefetch=1,
                grid=(2 * blocks,),
                in_specs=x_specs(count, blocks)
                + weight_specs(0, 1, blocks, widths)
                + [pl.BlockSpec((1, DEPTH), lambda k, *p: (0, jnp.minimum(k, blocks - 1)))],
                out_specs=[
                    pl.BlockSpec((count, width), lambda k, *p: (0, 0))
                    for width in (q_width, 2 * kv_width, HD, HD)
                ],
            ),
            out_shape=[
                whole((count, width), jnp.float32) for width in (q_width, 2 * kv_width, HD, HD)
            ],
            compiler_params=pltpu.CompilerParams(vmem_limit_bytes=56 << 20),
            cost_estimate=cost(count, 2 * part_width, columns),
            name="own_half",
        )(part, x, near, gain, *weights, value_head[None, :])

    def far_half(begin, places, far, far_near, sums, before):
        count = far.shape[0]
        tile = max(t for t in range(GRAIN, 209, GRAIN) if count % t == 0)
        fixed = lambda *shape: pl.BlockSpec(shape, lambda k, *p: (0, 0))
        return pl.pallas_call(
            functools.partial(second_kernel, slot, tile, begin),
            grid_spec=pltpu.PrefetchScalarGridSpec(
                num_scalar_prefetch=2,
                grid=(2 * blocks,),
                in_specs=x_specs(count, blocks)
                + weight_specs(2, 3, blocks, widths)
                + [fixed(count, width) for width in (q_width, 2 * kv_width, HD, HD)]
                + [fixed(slot, HD)] * 2
                + [fixed(q_width // HD, HD)]
                + [fixed(slot, HD)] * 2,
                out_specs=[fixed(count, HD), fixed(slot, HD), fixed(slot, HD)],
                scratch_shapes=[
                    pltpu.VMEM((count, q_width), jnp.float32),
                    pltpu.VMEM((count, 2 * kv_width), jnp.float32),
                    pltpu.VMEM((count, HD), jnp.float32),
                    pltpu.VMEM((count, HD), jnp.float32),
                    pltpu.VMEM((count, HD), jnp.float32),
                    pltpu.VMEM((count, HD), jnp.int32),
                    pltpu.VMEM((slot + count, HD), jnp.bfloat16),
                    pltpu.VMEM((slot + count, HD), jnp.bfloat16),
                ],
            ),
            out_shape=[
                whole((count, HD), jnp.float32),
                whole((slot, HD), jnp.bfloat16),
                whole((slot, HD), jnp.bfloat16),
            ],
            compiler_params=pltpu.CompilerParams(vmem_limit_bytes=56 << 20),
            cost_estimate=cost(count, 2 * part_width, columns),
            name="far_half",
        )(
            part, places, far, far_near, gain, *weights, *sums, cosine, sine,
            folded_head.reshape(q_width // HD, HD), *before,
        )

    x_first, places_first = pl.pallas_call(
        functools.partial(first_pack_kernel, slot_blocks),
        in_specs=[scalars, anywhere],
        out_specs=[onchip, scalars],
        out_shape=[whole((first, part_width), hidden.dtype), whole((blocks_in_all,), jnp.int32)],
        scratch_shapes=[
            pltpu.SMEM((blocks_in_all,), jnp.int32),
            pltpu.SemaphoreType.DMA((first // GRAIN,)),
        ],
        compiler_params=pltpu.CompilerParams(vmem_limit_bytes=32 << 20),
        name="first_pack",
    )(lengths, hidden)
    far_first = swapped(x_first, "mp", 2)

    owners = lax.axis_size("dp")
    me = lax.axis_index("dp").astype(jnp.int32)
    everyone = lax.psum(
        jnp.where(jnp.arange(owners)[:, None] == me, lengths[None, :], 0), "dp"
    ).reshape(-1)
    source, places, info, *ships = pl.pallas_call(
        functools.partial(
            plan_kernel, slot_blocks, first // GRAIN, (first + second) // GRAIN
        ),
        in_specs=[scalars, scalars, anywhere],
        out_specs=[scalars, scalars, scalars] + [onchip] * len(ROUTES),
        out_shape=[
            whole((blocks_in_all,), jnp.int32),
            whole((blocks_in_all,), jnp.int32),
            whole((64,), jnp.int32),
        ]
        + [whole((slot, part_width), hidden.dtype)] * len(ROUTES),
        scratch_shapes=[pltpu.SMEM((owners,), jnp.int32)] * 4
        + [pltpu.SemaphoreType.DMA((len(ROUTES),))],
        compiler_params=pltpu.CompilerParams(vmem_limit_bytes=32 << 20),
        name="plan",
    )(me[None], everyone, hidden)
    arrivals = [swapped(ship, "dp", bit) for ship, bit in zip(ships, ROUTES, strict=True)]

    def pack(begin, count):
        return pl.pallas_call(
            functools.partial(pack_kernel, begin, slot_blocks),
            in_specs=[scalars, anywhere] + [anywhere] * len(ROUTES),
            out_specs=onchip,
            out_shape=whole((count, part_width), hidden.dtype),
            scratch_shapes=[pltpu.SemaphoreType.DMA((count // GRAIN,))],
            compiler_params=pltpu.CompilerParams(vmem_limit_bytes=32 << 20),
            name="pack",
        )(source, hidden, *arrivals)

    nothing = jnp.zeros((slot, HD), jnp.bfloat16)
    sums_first = own_half(x_first)
    x_second = pack(first, second)
    far_second = swapped(x_second, "mp", 2)
    far_first, after = lax.optimization_barrier((far_first, sums_first[3]))
    total_first, *before = far_half(
        0, places_first, far_first, swapped(far_first, "mp", 1), sums_first, (nothing, nothing)
    )
    sums_second = own_half(x_second)
    far_second, _ = lax.optimization_barrier((far_second, (total_first, sums_second[3])))
    total_second, *before = far_half(
        first, places, far_second, swapped(far_second, "mp", 1), sums_second, before
    )

    def overflow(before):
        x = pack(first + second, rest)
        far = swapped(x, "mp", 2)
        return far_half(
            first + second, places, far, swapped(far, "mp", 1), own_half(x), before
        )[0]

    total_rest = lax.cond(
        info[OVERFLOW] > 0, overflow, lambda _: jnp.zeros((rest, HD), jnp.float32), before
    )
    terms = pl.pallas_call(
        functools.partial(unpack_kernel, slot, rollouts),
        in_specs=[scalars] + [onchip] * 3,
        out_shape=whole((rollouts + len(ROUTES), slot), jnp.float32),
        scratch_shapes=[pltpu.VMEM((rows + slot, HD), jnp.float32)],
        name="unpack",
    )(info, total_first, total_second, total_rest)

    slot_terms = terms[:rollouts]
    lanes = jnp.arange(rollouts, dtype=jnp.int32)
    for r, bit in enumerate(ROUTES):
        back = swapped(terms[rollouts + r], "dp", bit)
        mine = (lanes == info[SHIP_SLOT + r]) & (info[SHIPPED + r] > 0)
        slot_terms = jnp.where(mine[:, None], back[None, :], slot_terms)
    slot_values = lax.psum(slot_terms, "mp")

    step_ids = jnp.arange(slot, dtype=jnp.int32)
    live_mask = step_ids[None, :] < lengths[:, None]
    values = jnp.where(live_mask, slot_values, 0.0)
    next_live = step_ids[None, :] + 1 < lengths[:, None]
    following = jnp.concatenate([values[:, 1:], jnp.zeros((rollouts, 1), jnp.float32)], axis=1)
    one_step = jnp.where(
        live_mask, rewards + DISCOUNT * jnp.where(next_live, following, 0.0) - values, 0.0
    )
    lag_matrix = (step_ids[:, None] - step_ids[None, :]).astype(jnp.float32)
    decay_table = jnp.where(
        lag_matrix >= 0, jnp.exp(lag_matrix * math.log(DISCOUNT * SMOOTHING)), 0.0
    )
    advantages = jnp.dot(one_step, decay_table, precision=lax.Precision.HIGHEST)
    return (values, advantages)


def solution(mesh):
    return jax.shard_map(
        local,
        mesh=mesh,
        in_specs=(
            P("dp", "mp"),
            P("dp", None),
            P("dp"),
            P("dp"),
            P("dp"),
            P("dp"),
            P("dp"),
            P(),
            P(None, "mp"),
            P(None, "mp"),
            P(None, "mp"),
            P("mp"),
            P("mp"),
        ),
        out_specs=(P("dp", None), P("dp", None)),
        check_vma=False,
    )
```

```python
import functools
import math

import jax
import jax.numpy as jnp
from jax import lax
from jax.experimental import pallas as pl
from jax.experimental.pallas import tpu as pltpu
from jax.sharding import PartitionSpec as P

HD = 128
EPSILON = 1e-05
DISCOUNT = 0.99
SMOOTHING = 0.95
ROPE_BASE = 500000.0
DEPTH = 1024
PARTS = 4
GRAIN = 16
ROUTES = (1, 2, 4, 1)
BITS = (1, 2, 4)
SLOT_AT, ARRIVED_AT, SHIP_SLOT, SHIPPED, OVERFLOW = 0, 16, 24, 32, 40


def swapped(value, axis, bit):
    length = lax.axis_size(axis)
    return lax.ppermute(value, axis, [(i, i ^ bit) for i in range(length)])


def lane_groups(value):
    total = value[:, :HD]
    for at in range(HD, value.shape[1], HD):
        total = total + value[:, at : at + HD]
    return total


def add_products(x, gain_ref, wq_ref, wk_ref, wv_ref, q_acc, kv_acc, ss_acc, wkv):
    wkv[:, :HD] = wk_ref[...]
    wkv[:, HD:] = wv_ref[...]
    xf = x.astype(jnp.float32)
    ss_acc[...] += lane_groups(xf * xf)
    scaled = (xf * gain_ref[...]).astype(jnp.bfloat16)
    q_acc[...] += jnp.dot(scaled, wq_ref[...], preferred_element_type=jnp.float32)
    kv_acc[...] += jnp.dot(scaled, wkv[...], preferred_element_type=jnp.float32)


def by_part(step, blocks, x_refs, act):
    for f, refs in enumerate(x_refs):

        @pl.when((step >= f * blocks) & (step < (f + 1) * blocks))
        def _(f=f, refs=refs):
            act(f, refs)


def sums_kernel(parts, groups, begun, part_ref, *refs):
    refs = list(refs)
    take = lambda n: [refs.pop(0) for _ in range(n)]
    x_refs = [take(groups) for _ in range(parts)]
    weights = take(4)
    (head_ref,) = take(1)
    begun_refs = [take(4) for _ in range(groups)] if begun else None
    outs = [take(4) for _ in range(groups)]
    (wkv,) = take(1)
    step = pl.program_id(0)

    @pl.when(step == 0)
    def _():
        for g, out in enumerate(outs):
            for i, ref in enumerate(out):
                ref[...] = begun_refs[g][i][...] if begun else jnp.zeros_like(ref)

    def act(f, rows):
        for x_ref, (q_ref, kv_ref, ss_ref, vt_ref) in zip(rows, outs, strict=True):
            x = x_ref[...]
            if f == 0 and not begun:
                vt_ref[...] += lane_groups(x.astype(jnp.float32) * head_ref[...])
            add_products(x, *weights, q_ref, kv_ref, ss_ref, wkv)

    by_part(step, pl.num_programs(0) // parts, x_refs, act)


def turned(value, cosine, sine):
    return (value * cosine + pltpu.roll(value, HD // 2, 1) * sine).astype(jnp.bfloat16)


def attend_kernel(slot, tile, begin, parts, part_ref, place_ref, *refs):
    x_refs, refs = [[ref] for ref in refs[:parts]], refs[parts:]
    weights, refs = refs[:4], refs[4:]
    (
        q_ref, kv_ref, ss_ref, vt_ref, cos_ref, sin_ref, folded_ref, key_in, val_in,
        out_ref, key_out, val_out, q_acc, kv_acc, ss_acc, cos_rows, sin_rows, place_rows, keys, vals,
        queries, probs, wkv,
    ) = refs
    step = pl.program_id(0)
    steps = pl.num_programs(0)
    rows = q_acc.shape[0]
    heads = q_acc.shape[1] // HD

    @pl.when(step == 0)
    def _():
        q_acc[...] = q_ref[...]
        kv_acc[...] = kv_ref[...]
        ss_acc[...] = ss_ref[...]
        keys[:slot, :] = key_in[...]
        vals[:slot, :HD] = val_in[...]
        vals[:, HD:] = jnp.ones((slot + rows, HD), jnp.bfloat16)
        inner = lax.broadcasted_iota(jnp.int32, (GRAIN, HD), 0)

        def place(b, carry):
            at = place_ref[begin // GRAIN + b]
            here = pl.ds(pl.multiple_of(b * GRAIN, GRAIN), GRAIN)
            there = pl.ds(pl.multiple_of(at * GRAIN, GRAIN), GRAIN)
            cos_rows[here, :] = cos_ref[there, :]
            sin_rows[here, :] = sin_ref[there, :]
            place_rows[here, :] = inner + at * GRAIN
            return carry

        lax.fori_loop(0, rows // GRAIN, place, 0)

    def act(f, rows):
        add_products(rows[0][...], *weights, q_acc, kv_acc, ss_acc, wkv)

    by_part(step, steps // parts, x_refs, act)

    @pl.when(step == steps - 1)
    def _():
        features = DEPTH * steps // parts * PARTS
        scale = lax.rsqrt(jnp.sum(ss_acc[...], axis=1, keepdims=True) / features + EPSILON)
        keys[slot:, :] = turned(kv_acc[:, :HD] * scale, cos_rows[...], sin_rows[...])
        vals[slot:, :HD] = (kv_acc[:, HD:] * scale).astype(jnp.bfloat16)
        key_out[...] = keys[rows:, :]
        val_out[...] = vals[rows:, :HD]
        back = (
            lax.broadcasted_iota(jnp.int32, (tile, slot + tile), 0)
            + slot
            - lax.broadcasted_iota(jnp.int32, (tile, slot + tile), 1)
        )

        def one_tile(t, carry):
            here = pl.ds(pl.multiple_of(t * tile, GRAIN), tile)
            window = pl.ds(pl.multiple_of(t * tile, GRAIN), slot + tile)
            mean = jnp.sum(ss_acc[here, :], axis=1, keepdims=True) / features
            scale = lax.rsqrt(mean + EPSILON) * (math.log2(math.e) / math.sqrt(HD))
            cosine, sine = cos_rows[here, :] * scale, sin_rows[here, :] * scale
            bias = jnp.where((back >= 0) & (back <= place_rows[here, :1]), 0.0, -1e30)
            for h in range(heads):
                turned_h = turned(q_acc[here, h * HD : (h + 1) * HD], cosine, sine)
                queries[h * tile : (h + 1) * tile, :] = turned_h
            scores = lax.dot_general(
                queries[...], keys[window, :], (((1,), (1,)), ((), ())),
                preferred_element_type=jnp.float32,
            )
            for h in range(heads):
                score = scores[h * tile : (h + 1) * tile, :] + bias
                exps = jnp.exp2(score - jnp.max(score, axis=1, keepdims=True))
                probs[h * tile : (h + 1) * tile, :] = exps.astype(jnp.bfloat16)
            attended = jnp.dot(probs[...], vals[window, :], preferred_element_type=jnp.float32)
            total = vt_ref[here, :]
            for h in range(heads):
                mine = attended[h * tile : (h + 1) * tile, :]
                total = total + mine[:, :HD] / mine[:, HD:] * folded_ref[h : h + 1, :]
            out_ref[here, :] = total
            return carry

        lax.fori_loop(0, rows // tile, one_tile, 0, unroll=2)


def start_copy(source, source_block, target, target_block, sem):
    pltpu.make_async_copy(
        source.at[pl.ds(pl.multiple_of(source_block * GRAIN, GRAIN), GRAIN)],
        target.at[pl.ds(pl.multiple_of(target_block * GRAIN, GRAIN), GRAIN)],
        sem,
    ).start()


def wait_copies(source, targets, sems):
    begin = 0
    for target in targets:

        def wait(b, carry, target=target, begin=begin):
            pltpu.make_async_copy(
                source.at[pl.ds(0, GRAIN)],
                target.at[pl.ds(pl.multiple_of(b * GRAIN, GRAIN), GRAIN)],
                sems.at[begin + b],
            ).wait()
            return carry

        lax.fori_loop(0, target.shape[0] // GRAIN, wait, 0)
        begin += target.shape[0] // GRAIN


def blocks_of(length):
    return (length + (GRAIN - 1)) >> (GRAIN.bit_length() - 1)


def lay_out(begin, count, slot_blocks, first_block, source_ref, place_ref):
    def enter(j, carry):
        source_ref[begin + j] = first_block + j
        place_ref[begin + j] = j
        return carry

    lax.fori_loop(0, count, enter, 0)


def lay_out_fill(slot_blocks, source_ref, place_ref):
    def enter(b, carry):
        source_ref[b] = b
        place_ref[b] = lax.rem(b, slot_blocks)
        return carry

    lax.fori_loop(0, source_ref.shape[0], enter, 0)


def first_pack_kernel(slot_blocks, lengths_ref, hidden_ref, place_ref, *refs):
    outs, (source_ref, sems) = refs[:-2], refs[-2:]
    lay_out_fill(slot_blocks, source_ref, place_ref)
    at = jnp.int32(0)
    for i in range(lengths_ref.shape[0]):
        count = blocks_of(lengths_ref[i])
        lay_out(at, count, slot_blocks, i * slot_blocks, source_ref, place_ref)
        at = at + count
    begin = 0
    for out_ref in outs:

        def start(b, carry, out_ref=out_ref, begin=begin):
            start_copy(hidden_ref, source_ref[begin + b], out_ref, b, sems.at[begin + b])
            return carry

        lax.fori_loop(0, out_ref.shape[0] // GRAIN, start, 0)
        begin += out_ref.shape[0] // GRAIN
    wait_copies(hidden_ref, outs, sems)


def plan_kernel(
    slot_blocks, first_blocks, capacity, me_ref, lengths_ref, hidden_ref,
    source_ref, place_ref, info_ref, *refs,
):
    kept, load, sent, moved, sems = refs[len(BITS) :]
    size = slot_blocks * GRAIN
    ships = [
        refs[BITS.index(bit)].at[pl.ds(ROUTES[:r].count(bit) * size, size)]
        for r, bit in enumerate(ROUTES)
    ]
    me = me_ref[0]
    owners = kept.shape[0]
    rollouts = lengths_ref.shape[0] // owners

    def begin(o, carry):
        total = jnp.int32(0)
        for i in range(rollouts):
            total = total + blocks_of(lengths_ref[o * rollouts + i])
        kept[o] = total
        load[o] = jnp.maximum(total, first_blocks)
        sent[o] = 0
        return carry

    lax.fori_loop(0, owners, begin, 0)
    arrived = []
    for r, bit in enumerate(ROUTES):

        def choose(o, carry):
            count = blocks_of(lengths_ref[o * rollouts + rollouts - 1 - sent[o]])
            useful = (kept[o] - count >= first_blocks) & (load[o ^ bit] + count < load[o])
            moved[o] = jnp.where(useful, count, 0)
            return carry

        lax.fori_loop(0, owners, choose, 0)
        slot_now = rollouts - 1 - sent[me]
        info_ref[SHIP_SLOT + r] = slot_now
        info_ref[SHIPPED + r] = jnp.where(moved[me] > 0, 1, 0)
        arrived.append(moved[me ^ bit])
        pltpu.make_async_copy(
            hidden_ref.at[pl.ds(pl.multiple_of(slot_now * size, GRAIN), size)],
            ships[r],
            sems.at[r],
        ).start()

        def move(o, carry):
            kept[o] = kept[o] - moved[o]
            load[o] = load[o] - moved[o] + moved[o ^ bit]
            sent[o] = sent[o] + jnp.where(moved[o] > 0, 1, 0)
            return carry

        lax.fori_loop(0, owners, move, 0)

    most = lax.fori_loop(0, owners, lambda o, m: jnp.maximum(m, load[o]), jnp.int32(0))
    info_ref[OVERFLOW] = jnp.where(most > capacity, 1, 0)

    lay_out_fill(slot_blocks, source_ref, place_ref)
    at = jnp.int32(0)
    for i in range(rollouts):
        here = i < rollouts - sent[me]
        count = jnp.where(here, blocks_of(lengths_ref[me * rollouts + i]), 0)
        info_ref[SLOT_AT + i] = jnp.where(here, at, 0)
        lay_out(at, count, slot_blocks, i * slot_blocks, source_ref, place_ref)
        at = at + count
    at = jnp.maximum(at, first_blocks)
    for r in range(len(ROUTES)):
        info_ref[ARRIVED_AT + r] = jnp.where(arrived[r] > 0, at, 0)
        lay_out(at, arrived[r], slot_blocks, (rollouts + r) * slot_blocks, source_ref, place_ref)
        at = at + arrived[r]
    for r in range(len(ROUTES)):
        pltpu.make_async_copy(hidden_ref.at[pl.ds(0, size)], ships[r], sems.at[r]).wait()


def pack_kernel(begin, slot_blocks, source_ref, hidden_ref, *refs):
    outs, sems = refs[len(BITS) : -1], refs[-1]
    size = slot_blocks * GRAIN
    arrivals = [
        refs[BITS.index(bit)].at[pl.ds(ROUTES[:r].count(bit) * size, size)]
        for r, bit in enumerate(ROUTES)
    ]
    own = hidden_ref.shape[0] // GRAIN
    done = 0
    for out_ref in outs:

        def start(b, carry, out_ref=out_ref, done=done):
            block = source_ref[begin // GRAIN + done + b]

            @pl.when(block < own)
            def _():
                start_copy(hidden_ref, block, out_ref, b, sems.at[done + b])

            for r, arrival in enumerate(arrivals):
                low = own + r * slot_blocks

                @pl.when((block >= low) & (block < low + slot_blocks))
                def _(arrival=arrival, low=low):
                    start_copy(arrival, block - low, out_ref, b, sems.at[done + b])

            return carry

        lax.fori_loop(0, out_ref.shape[0] // GRAIN, start, 0)
        done += out_ref.shape[0] // GRAIN
    wait_copies(hidden_ref, outs, sems)


def unpack_kernel(slot, rollouts, info_ref, *refs):
    totals, out_ref, back_refs, rows_ref = refs[:3], refs[3], refs[4:-1], refs[-1]
    at = 0
    for total in totals:
        rows_ref[at : at + total.shape[0], :] = total[...]
        at += total.shape[0]
    rows_ref[at:, :] = jnp.zeros((rows_ref.shape[0] - at, HD), jnp.float32)
    span = rows_ref.shape[0] - at

    def line(block):
        part = rows_ref[pl.ds(pl.multiple_of(block * GRAIN, GRAIN), span), :]
        return jnp.sum(part.T, axis=0, keepdims=True)[:, :slot]

    for i in range(rollouts):
        out_ref[i : i + 1, :] = line(info_ref[SLOT_AT + i])
    for r, bit in enumerate(ROUTES):
        back_ref, i = back_refs[BITS.index(bit)], ROUTES[:r].count(bit)
        back_ref[i : i + 1, :] = line(info_ref[ARRIVED_AT + r])


def weight_specs(flips, blocks, widths):
    def row(step, part_ref, *rest):
        flip = flips[0]
        for f in range(1, len(flips)):
            flip = jnp.where(step < f * blocks, flip, flips[f])
        return (part_ref[0] ^ flip) * blocks + lax.rem(step, blocks)

    return [pl.BlockSpec((1, DEPTH), lambda k, *p: (0, row(k, *p)))] + [
        pl.BlockSpec((DEPTH, width), lambda k, *p: (row(k, *p), 0)) for width in widths
    ]


def x_spec(rows, blocks, f):
    return pl.BlockSpec((rows, DEPTH), lambda k, *p: (0, jnp.clip(k - f * blocks, 0, blocks - 1)))


def fixed(*shape):
    return pl.BlockSpec(shape, lambda k, *p: (0, 0))


def cost(rows, depth, columns):
    return pl.CostEstimate(
        flops=2 * rows * depth * columns,
        bytes_accessed=2 * depth * (rows + columns) + 4 * rows * columns,
        transcendentals=0,
    )


def sums_call(shared, flips, xs, head, begun=None):
    part, gain, weights = shared
    widths = [w.shape[1] for w in weights]
    groups = len(xs[0])
    blocks = xs[0][0].shape[1] // DEPTH
    counts = [x.shape[0] for x in xs[0]]
    outs = [(count, width) for count in counts for width in (widths[0], sum(widths[1:]), HD, HD)]
    given = [a for group in begun for a in group] if begun else []
    sums = pl.pallas_call(
        functools.partial(sums_kernel, len(flips), groups, begun is not None),
        grid_spec=pltpu.PrefetchScalarGridSpec(
            num_scalar_prefetch=1,
            grid=(len(flips) * blocks,),
            in_specs=[x_spec(count, blocks, f) for f in range(len(flips)) for count in counts]
            + weight_specs(flips, blocks, widths)
            + [pl.BlockSpec((1, DEPTH), lambda k, *p: (0, jnp.minimum(k, blocks - 1)))]
            + [fixed(*a.shape) for a in given],
            out_specs=[fixed(*shape) for shape in outs],
            scratch_shapes=[pltpu.VMEM((DEPTH, 2 * HD), jnp.bfloat16)],
        ),
        out_shape=[jax.ShapeDtypeStruct(shape, jnp.float32) for shape in outs],
        compiler_params=pltpu.CompilerParams(vmem_limit_bytes=24 << 20),
        cost_estimate=cost(sum(counts), len(flips) * blocks * DEPTH, sum(widths)),
        name="sums",
    )(part, *[x for row in xs for x in row], gain, *weights, head, *given)
    return [sums[4 * g : 4 * g + 4] for g in range(groups)]


def attend_call(shared, tables, begin, places, flips, xs, sums, before):
    part, gain, weights = shared
    widths = [w.shape[1] for w in weights]
    count, blocks = xs[0].shape[0], xs[0].shape[1] // DEPTH
    slot = tables[0].shape[0]
    tile = max(t for t in range(GRAIN, slot // 2 + 1, GRAIN) if count % t == 0)
    stacked = widths[0] // HD * tile
    return pl.pallas_call(
        functools.partial(attend_kernel, slot, tile, begin, len(flips)),
        grid_spec=pltpu.PrefetchScalarGridSpec(
            num_scalar_prefetch=2,
            grid=(len(flips) * blocks,),
            in_specs=[x_spec(count, blocks, f) for f in range(len(flips))]
            + weight_specs(flips, blocks, widths)
            + [fixed(*a.shape) for a in (*sums, *tables, *before)],
            out_specs=[fixed(count, HD), fixed(slot, HD), fixed(slot, HD)],
            scratch_shapes=[
                pltpu.VMEM((count, widths[0]), jnp.float32),
                pltpu.VMEM((count, widths[1] + widths[2]), jnp.float32),
                pltpu.VMEM((count, HD), jnp.float32),
                pltpu.VMEM((count, HD), jnp.float32),
                pltpu.VMEM((count, HD), jnp.float32),
                pltpu.VMEM((count, HD), jnp.int32),
                pltpu.VMEM((slot + count, HD), jnp.bfloat16),
                pltpu.VMEM((slot + count, 2 * HD), jnp.bfloat16),
                pltpu.VMEM((stacked, HD), jnp.bfloat16),
                pltpu.VMEM((stacked, slot + tile), jnp.bfloat16),
                pltpu.VMEM((DEPTH, 2 * HD), jnp.bfloat16),
            ],
        ),
        out_shape=[
            jax.ShapeDtypeStruct((count, HD), jnp.float32),
            jax.ShapeDtypeStruct((slot, HD), jnp.bfloat16),
            jax.ShapeDtypeStruct((slot, HD), jnp.bfloat16),
        ],
        compiler_params=pltpu.CompilerParams(vmem_limit_bytes=24 << 20),
        cost_estimate=cost(count, len(flips) * blocks * DEPTH, sum(widths)),
        name="attend",
    )(part, places, *xs, gain, *weights, *sums, *tables, *before)


def local(
    hidden,
    rewards,
    lengths,
    dest_shard,
    source_owner,
    pack_offset,
    segment_ids,
    norm_gain,
    w_query,
    w_key,
    w_value,
    value_head,
    folded_head,
):
    rollouts, slot = rewards.shape
    rows, part_width = hidden.shape
    q_width = w_query.shape[1]
    part = lax.axis_index("mp").astype(jnp.int32)[None]
    gain = norm_gain[None, :]
    weights = (w_query, w_key, w_value)

    positions = jnp.arange(slot, dtype=jnp.float32)
    half = HD // 2
    frequency = ROPE_BASE ** (-jnp.arange(half, dtype=jnp.float32) / half)
    angles = positions[:, None] * frequency[None, :]
    cosine = jnp.concatenate([jnp.cos(angles)] * 2, axis=1)
    sine = jnp.concatenate([-jnp.sin(angles), jnp.sin(angles)], axis=1)

    slot_blocks = slot // GRAIN
    packed = segment_ids.shape[0]
    first = packed * 4 // 5
    second = packed * 3 // 5
    rest = rows - first - second
    whole = jax.ShapeDtypeStruct
    anywhere = pl.BlockSpec(memory_space=pl.ANY)
    scalars = pl.BlockSpec(memory_space=pltpu.SMEM)
    onchip = pl.BlockSpec(memory_space=pltpu.VMEM)
    blocks_in_all = rows // GRAIN
    shared = (part, gain, weights)
    head = value_head[None, :]
    tables = (cosine, sine, folded_head.reshape(q_width // HD, HD))
    vmem = pltpu.CompilerParams(vmem_limit_bytes=12 << 20)

    places_first, x_first = pl.pallas_call(
        functools.partial(first_pack_kernel, slot_blocks),
        in_specs=[scalars, anywhere],
        out_specs=[scalars, onchip],
        out_shape=[whole((blocks_in_all,), jnp.int32), whole((first, part_width), hidden.dtype)],
        scratch_shapes=[
            pltpu.SMEM((blocks_in_all,), jnp.int32),
            pltpu.SemaphoreType.DMA((first // GRAIN,)),
        ],
        compiler_params=vmem,
        name="first_pack",
    )(lengths, hidden)
    far_first = swapped(x_first, "mp", 2)
    near_first = swapped(x_first, "mp", 1)

    owners = lax.axis_size("dp")
    me = lax.axis_index("dp").astype(jnp.int32)
    everyone = lax.psum(
        jnp.where(jnp.arange(owners)[:, None] == me, lengths[None, :], 0), "dp"
    ).reshape(-1)
    source, places, info, *ships = pl.pallas_call(
        functools.partial(
            plan_kernel, slot_blocks, first // GRAIN, (first + second) // GRAIN
        ),
        in_specs=[scalars, scalars, anywhere],
        out_specs=[scalars, scalars, scalars] + [onchip] * len(BITS),
        out_shape=[
            whole((blocks_in_all,), jnp.int32),
            whole((blocks_in_all,), jnp.int32),
            whole((64,), jnp.int32),
        ]
        + [whole((ROUTES.count(bit) * slot, part_width), hidden.dtype) for bit in BITS],
        scratch_shapes=[pltpu.SMEM((owners,), jnp.int32)] * 4
        + [pltpu.SemaphoreType.DMA((len(ROUTES),))],
        compiler_params=vmem,
        name="plan",
    )(me[None], everyone, hidden)
    arrivals = [swapped(ship, "dp", bit) for ship, bit in zip(ships, BITS, strict=True)]

    shipped = info[SHIPPED : SHIPPED + len(ROUTES)] > 0
    ship_slots = info[SHIP_SLOT : SHIP_SLOT + len(ROUTES)]
    mine = shipped[:, None] & (ship_slots[:, None] == jnp.arange(rollouts)[None, :])

    def pack(begin, count):
        return pl.pallas_call(
            functools.partial(pack_kernel, begin, slot_blocks),
            in_specs=[scalars, anywhere] + [anywhere] * len(BITS),
            out_specs=onchip,
            out_shape=whole((count, part_width), hidden.dtype),
            scratch_shapes=[pltpu.SemaphoreType.DMA((count // GRAIN,))],
            compiler_params=vmem,
            name="pack",
        )(source, hidden, *arrivals)

    def attend(begin, places, far, sums, before):
        return attend_call(
            shared, tables, begin, places, (2, 3), [far, swapped(far, "mp", 1)], sums, before
        )

    nothing = jnp.zeros((slot, HD), jnp.bfloat16)
    before = (nothing, nothing)
    (sums_first,) = sums_call(shared, (0, 1), [[x_first], [near_first]], head)
    far_first, mine, sums_first, *arrivals = lax.optimization_barrier(
        (far_first, mine, sums_first, *arrivals)
    )
    x_second = pack(first, second)
    far_second = swapped(x_second, "mp", 2)
    near_second = swapped(x_second, "mp", 1)
    total_first, *before = attend(0, places_first, far_first, sums_first, before)
    x_second, near_second, _ = lax.optimization_barrier((x_second, near_second, total_first))
    (sums_second,) = sums_call(shared, (0, 1), [[x_second], [near_second]], head)
    far_second, sums_second = lax.optimization_barrier((far_second, sums_second))
    far_near = swapped(far_second, "mp", 1)
    (sums_second,) = sums_call(shared, (2,), [[far_second]], head, begun=[sums_second])
    far_near, sums_second = lax.optimization_barrier((far_near, sums_second))
    total_second, *before = attend_call(
        shared, tables, first, places, (3,), [far_near], sums_second, before
    )

    def overflow(before):
        begin = first + second
        x = pack(begin, rest)
        (sums,) = sums_call(shared, (0, 1), [[x], [swapped(x, "mp", 1)]], head)
        return attend(begin, places, swapped(x, "mp", 2), sums, before)[0]

    total_rest = lax.cond(
        info[OVERFLOW] > 0, overflow, lambda _: jnp.zeros((rest, HD), jnp.float32), before
    )
    totals = (total_first, total_second, total_rest)
    slot_terms, *backs = pl.pallas_call(
        functools.partial(unpack_kernel, slot, rollouts),
        in_specs=[scalars] + [onchip] * len(totals),
        out_shape=[whole((rollouts, slot), jnp.float32)]
        + [whole((ROUTES.count(bit), slot), jnp.float32) for bit in BITS],
        scratch_shapes=[pltpu.VMEM((rows + 2 * HD, HD), jnp.float32)],
        name="unpack",
    )(info, *totals)
    backs = [swapped(back, "dp", bit) for back, bit in zip(backs, BITS, strict=True)]
    for r, bit in enumerate(ROUTES):
        back = backs[BITS.index(bit)][ROUTES[:r].count(bit)]
        slot_terms = jnp.where(mine[r, :, None], back[None, :], slot_terms)
    slot_values = slot_terms
    for bit in (1, 2):
        slot_values = slot_values + swapped(slot_values, "mp", bit)

    step_ids = jnp.arange(slot, dtype=jnp.int32)
    live_mask = step_ids[None, :] < lengths[:, None]
    values = jnp.where(live_mask, slot_values, 0.0)
    next_live = step_ids[None, :] + 1 < lengths[:, None]
    following = jnp.concatenate([values[:, 1:], jnp.zeros((rollouts, 1), jnp.float32)], axis=1)
    one_step = jnp.where(
        live_mask, rewards + DISCOUNT * jnp.where(next_live, following, 0.0) - values, 0.0
    )
    lag_matrix = (step_ids[:, None] - step_ids[None, :]).astype(jnp.float32)
    decay_table = jnp.where(
        lag_matrix >= 0, jnp.exp(lag_matrix * math.log(DISCOUNT * SMOOTHING)), 0.0
    )
    advantages = jnp.dot(one_step, decay_table, precision=lax.Precision.HIGHEST)
    return (values, advantages)


def solution(mesh):
    return jax.shard_map(
        local,
        mesh=mesh,
        in_specs=(
            P("dp", "mp"),
            P("dp", None),
            P("dp"),
            P("dp"),
            P("dp"),
            P("dp"),
            P("dp"),
            P(),
            P(None, "mp"),
            P(None, "mp"),
            P(None, "mp"),
            P("mp"),
            P("mp"),
        ),
        out_specs=(P("dp", None), P("dp", None)),
        check_vma=False,
    )
```

```python
import functools
import math

import jax
import jax.numpy as jnp
from jax import lax
from jax.experimental import pallas as pl
from jax.experimental.pallas import tpu as pltpu
from jax.sharding import PartitionSpec as P

HD = 128
EPSILON = 1e-05
DISCOUNT = 0.99
SMOOTHING = 0.95
ROPE_BASE = 500000.0
DEPTH = 1024
PARTS = 4
GRAIN = 16
ROUTES = (1, 2, 4, 1)
BITS = (1, 2, 4)
SLOT_AT, ARRIVED_AT, SHIP_SLOT, SHIPPED, OVERFLOW = 0, 16, 24, 32, 40


def swapped(value, axis, bit):
    length = lax.axis_size(axis)
    return lax.ppermute(value, axis, [(i, i ^ bit) for i in range(length)])


def lane_groups(value):
    total = value[:, :HD]
    for at in range(HD, value.shape[1], HD):
        total = total + value[:, at : at + HD]
    return total


def add_products(x, gain_ref, wq_ref, wk_ref, wv_ref, q_acc, kv_acc, ss_acc, wkv):
    wkv[:, :HD] = wk_ref[...]
    wkv[:, HD:] = wv_ref[...]
    xf = x.astype(jnp.float32)
    ss_acc[...] += lane_groups(xf * xf)
    scaled = (xf * gain_ref[...]).astype(jnp.bfloat16)
    q_acc[...] += jnp.dot(scaled, wq_ref[...], preferred_element_type=jnp.float32)
    kv_acc[...] += jnp.dot(scaled, wkv[...], preferred_element_type=jnp.float32)


def by_part(step, blocks, x_refs, act):
    for f, refs in enumerate(x_refs):

        @pl.when((step >= f * blocks) & (step < (f + 1) * blocks))
        def _(f=f, refs=refs):
            act(f, refs)


def sums_kernel(parts, groups, begun, part_ref, *refs):
    refs = list(refs)
    take = lambda n: [refs.pop(0) for _ in range(n)]
    x_refs = [take(groups) for _ in range(parts)]
    weights = take(4)
    (head_ref,) = take(1)
    begun_refs = [take(4) for _ in range(groups)] if begun else None
    outs = [take(4) for _ in range(groups)]
    (wkv,) = take(1)
    step = pl.program_id(0)

    @pl.when(step == 0)
    def _():
        for g, out in enumerate(outs):
            for i, ref in enumerate(out):
                ref[...] = begun_refs[g][i][...] if begun else jnp.zeros_like(ref)

    def act(f, rows):
        for x_ref, (q_ref, kv_ref, ss_ref, vt_ref) in zip(rows, outs, strict=True):
            x = x_ref[...]
            if f == 0 and not begun:
                vt_ref[...] += lane_groups(x.astype(jnp.float32) * head_ref[...])
            add_products(x, *weights, q_ref, kv_ref, ss_ref, wkv)

    by_part(step, pl.num_programs(0) // parts, x_refs, act)


def turned(value, cosine, sine):
    return (value * cosine + pltpu.roll(value, HD // 2, 1) * sine).astype(jnp.bfloat16)


def attend_kernel(slot, tile, begin, parts, last, part_ref, place_ref, *refs):
    if last:
        info_ref, refs = refs[0], refs[1:]
    x_refs, refs = [[ref] for ref in refs[:parts]], refs[parts:]
    weights, refs = refs[:4], refs[4:]
    if last:
        (total_ref, line_ref, *back_refs, rows_ref), refs = refs[-3 - len(BITS) :], refs[: -3 - len(BITS)]
    (
        q_ref, kv_ref, ss_ref, vt_ref, cos_ref, sin_ref, folded_ref, key_in, val_in,
        out_ref, key_out, val_out, q_acc, kv_acc, ss_acc, cos_rows, sin_rows, place_rows, keys, vals,
        queries, probs, wkv,
    ) = refs
    step = pl.program_id(0)
    steps = pl.num_programs(0)
    rows = q_acc.shape[0]
    heads = q_acc.shape[1] // HD

    @pl.when(step == 0)
    def _():
        q_acc[...] = q_ref[...]
        kv_acc[...] = kv_ref[...]
        ss_acc[...] = ss_ref[...]
        keys[:slot, :] = key_in[...]
        vals[:slot, :HD] = val_in[...]
        vals[:, HD:] = jnp.ones((slot + rows, HD), jnp.bfloat16)
        inner = lax.broadcasted_iota(jnp.int32, (GRAIN, HD), 0)

        def place(b, carry):
            at = place_ref[begin // GRAIN + b]
            here = pl.ds(pl.multiple_of(b * GRAIN, GRAIN), GRAIN)
            there = pl.ds(pl.multiple_of(at * GRAIN, GRAIN), GRAIN)
            cos_rows[here, :] = cos_ref[there, :]
            sin_rows[here, :] = sin_ref[there, :]
            place_rows[here, :] = inner + at * GRAIN
            return carry

        lax.fori_loop(0, rows // GRAIN, place, 0)

    def act(f, rows):
        add_products(rows[0][...], *weights, q_acc, kv_acc, ss_acc, wkv)

    by_part(step, steps // parts, x_refs, act)

    @pl.when(step == steps - 1)
    def _():
        features = DEPTH * steps // parts * PARTS
        scale = lax.rsqrt(jnp.sum(ss_acc[...], axis=1, keepdims=True) / features + EPSILON)
        keys[slot:, :] = turned(kv_acc[:, :HD] * scale, cos_rows[...], sin_rows[...])
        vals[slot:, :HD] = (kv_acc[:, HD:] * scale).astype(jnp.bfloat16)
        key_out[...] = keys[rows:, :]
        val_out[...] = vals[rows:, :HD]
        back = (
            lax.broadcasted_iota(jnp.int32, (tile, slot + tile), 0)
            + slot
            - lax.broadcasted_iota(jnp.int32, (tile, slot + tile), 1)
        )

        def one_tile(t, carry):
            here = pl.ds(pl.multiple_of(t * tile, GRAIN), tile)
            window = pl.ds(pl.multiple_of(t * tile, GRAIN), slot + tile)
            mean = jnp.sum(ss_acc[here, :], axis=1, keepdims=True) / features
            scale = lax.rsqrt(mean + EPSILON) * (math.log2(math.e) / math.sqrt(HD))
            cosine, sine = cos_rows[here, :] * scale, sin_rows[here, :] * scale
            bias = jnp.where((back >= 0) & (back <= place_rows[here, :1]), 0.0, -1e30)
            for h in range(heads):
                turned_h = turned(q_acc[here, h * HD : (h + 1) * HD], cosine, sine)
                queries[h * tile : (h + 1) * tile, :] = turned_h
            scores = lax.dot_general(
                queries[...], keys[window, :], (((1,), (1,)), ((), ())),
                preferred_element_type=jnp.float32,
            )
            for h in range(heads):
                score = scores[h * tile : (h + 1) * tile, :] + bias
                exps = jnp.exp2(score - jnp.max(score, axis=1, keepdims=True))
                probs[h * tile : (h + 1) * tile, :] = exps.astype(jnp.bfloat16)
            attended = jnp.dot(probs[...], vals[window, :], preferred_element_type=jnp.float32)
            total = vt_ref[here, :]
            for h in range(heads):
                mine = attended[h * tile : (h + 1) * tile, :]
                total = total + mine[:, :HD] / mine[:, HD:] * folded_ref[h : h + 1, :]
            out_ref[here, :] = total
            return carry

        lax.fori_loop(0, rows // tile, one_tile, 0, unroll=2)
        if last:
            rows_ref[:begin, :] = total_ref[...]
            rows_ref[begin : begin + rows, :] = out_ref[...]
            unpack(slot, info_ref, rows_ref, line_ref, back_refs)


def start_copy(source, source_block, target, target_block, sem):
    pltpu.make_async_copy(
        source.at[pl.ds(pl.multiple_of(source_block * GRAIN, GRAIN), GRAIN)],
        target.at[pl.ds(pl.multiple_of(target_block * GRAIN, GRAIN), GRAIN)],
        sem,
    ).start()


def wait_copies(source, target, sem):
    pltpu.make_async_copy(source.at[pl.ds(0, target.shape[0])], target, sem).wait()


def blocks_of(length):
    return (length + (GRAIN - 1)) >> (GRAIN.bit_length() - 1)


def lay_out(begin, count, slot_blocks, first_block, source_ref, place_ref):
    def enter(j, carry):
        source_ref[begin + j] = first_block + j
        place_ref[begin + j] = j
        return carry

    lax.fori_loop(0, count, enter, 0)


def lay_out_fill(slot_blocks, source_ref, place_ref):
    def enter(b, carry):
        source_ref[b] = b
        place_ref[b] = lax.rem(b, slot_blocks)
        return carry

    lax.fori_loop(0, source_ref.shape[0], enter, 0)


def first_pack_kernel(slot_blocks, lengths_ref, hidden_ref, place_ref, out_ref, sem):
    total = out_ref.shape[0] // GRAIN

    def copy(j, carry, at, first_block):
        start_copy(hidden_ref, first_block + j, out_ref, at + j, sem)
        place_ref[at + j] = j
        return carry

    at = jnp.int32(0)
    for i in range(lengths_ref.shape[0]):
        count = jnp.minimum(blocks_of(lengths_ref[i]), total - at)
        lax.fori_loop(0, count, functools.partial(copy, at=at, first_block=i * slot_blocks), 0)
        at = at + count

    def fill(b, carry):
        start_copy(hidden_ref, 0, out_ref, b, sem)
        place_ref[b] = 0
        return carry

    lax.fori_loop(at, total, fill, 0)
    wait_copies(hidden_ref, out_ref, sem)


def plan_kernel(
    slot_blocks, first_blocks, capacity, extra, me_ref, lengths_ref, hidden_ref,
    source_ref, place_ref, info_ref, *refs,
):
    kept, load, sent, moved, sems = refs[len(BITS) :]
    size = slot_blocks * GRAIN
    ships = [
        refs[BITS.index(bit)].at[pl.ds(ROUTES[:r].count(bit) * size, size)]
        for r, bit in enumerate(ROUTES)
    ]
    me = me_ref[0]
    owners = kept.shape[0]
    rollouts = lengths_ref.shape[0] // owners

    def begin(o, carry):
        total = jnp.int32(0)
        for i in range(rollouts):
            total = total + blocks_of(lengths_ref[o * rollouts + i])
        kept[o] = total
        load[o] = jnp.maximum(total, first_blocks)
        sent[o] = 0
        return carry

    lax.fori_loop(0, owners, begin, 0)
    arrived = []
    for r, bit in enumerate(ROUTES):

        def choose(o, carry):
            count = blocks_of(lengths_ref[o * rollouts + rollouts - 1 - sent[o]])
            useful = (kept[o] - count >= first_blocks) & (load[o ^ bit] + count < load[o])
            moved[o] = jnp.where(useful, count, 0)
            return carry

        lax.fori_loop(0, owners, choose, 0)
        slot_now = rollouts - 1 - sent[me]
        info_ref[SHIP_SLOT + r] = slot_now
        info_ref[SHIPPED + r] = jnp.where(moved[me] > 0, 1, 0)
        arrived.append(moved[me ^ bit])
        pltpu.make_async_copy(
            hidden_ref.at[pl.ds(pl.multiple_of(slot_now * size, GRAIN), size)],
            ships[r],
            sems.at[r],
        ).start()

        def move(o, carry):
            kept[o] = kept[o] - moved[o]
            load[o] = load[o] - moved[o] + moved[o ^ bit]
            sent[o] = sent[o] + jnp.where(moved[o] > 0, 1, 0)
            return carry

        lax.fori_loop(0, owners, move, 0)

    most = lax.fori_loop(0, owners, lambda o, m: jnp.maximum(m, load[o]), jnp.int32(0))
    more = jnp.where(most > capacity + extra, 2, 1)
    info_ref[OVERFLOW] = jnp.where(most > capacity, more, 0)

    lay_out_fill(slot_blocks, source_ref, place_ref)
    at = jnp.int32(0)
    for i in range(rollouts):
        here = i < rollouts - sent[me]
        count = jnp.where(here, blocks_of(lengths_ref[me * rollouts + i]), 0)
        info_ref[SLOT_AT + i] = jnp.where(here, at, 0)
        lay_out(at, count, slot_blocks, i * slot_blocks, source_ref, place_ref)
        at = at + count
    at = jnp.maximum(at, first_blocks)
    for r in range(len(ROUTES)):
        info_ref[ARRIVED_AT + r] = jnp.where(arrived[r] > 0, at, 0)
        lay_out(at, arrived[r], slot_blocks, (rollouts + r) * slot_blocks, source_ref, place_ref)
        at = at + arrived[r]
    for r in range(len(ROUTES)):
        pltpu.make_async_copy(hidden_ref.at[pl.ds(0, size)], ships[r], sems.at[r]).wait()


def pack_kernel(begin, slot_blocks, source_ref, hidden_ref, *refs):
    out_ref, sem = refs[len(BITS) :]
    size = slot_blocks * GRAIN
    arrivals = [
        refs[BITS.index(bit)].at[pl.ds(ROUTES[:r].count(bit) * size, size)]
        for r, bit in enumerate(ROUTES)
    ]
    own = hidden_ref.shape[0] // GRAIN

    def start(b, carry):
        block = source_ref[begin // GRAIN + b]

        @pl.when(block < own)
        def _():
            start_copy(hidden_ref, block, out_ref, b, sem)

        for r, arrival in enumerate(arrivals):
            low = own + r * slot_blocks

            @pl.when((block >= low) & (block < low + slot_blocks))
            def _(arrival=arrival, low=low):
                start_copy(arrival, block - low, out_ref, b, sem)

        return carry

    lax.fori_loop(0, out_ref.shape[0] // GRAIN, start, 0)
    wait_copies(hidden_ref, out_ref, sem)


def unpack(slot, info_ref, rows_ref, out_ref, back_refs):
    rollouts = out_ref.shape[0]

    def line(block):
        part = rows_ref[pl.ds(pl.multiple_of(block * GRAIN, GRAIN), 2 * HD), :]
        return jnp.sum(part.T, axis=0, keepdims=True)[:, :slot]

    for i in range(rollouts):
        out_ref[i : i + 1, :] = line(info_ref[SLOT_AT + i])
    for r, bit in enumerate(ROUTES):
        back_ref, i = back_refs[BITS.index(bit)], ROUTES[:r].count(bit)
        back_ref[i : i + 1, :] = line(info_ref[ARRIVED_AT + r])


def unpack_kernel(slot, info_ref, *refs):
    totals, out_ref, back_refs, rows_ref = refs[:3], refs[3], refs[4:-1], refs[-1]
    at = 0
    for total in totals:
        rows_ref[at : at + total.shape[0], :] = total[...]
        at += total.shape[0]
    rows_ref[at:, :] = jnp.zeros((rows_ref.shape[0] - at, HD), jnp.float32)
    unpack(slot, info_ref, rows_ref, out_ref, back_refs)


def line_shapes(rollouts, slot):
    return [jax.ShapeDtypeStruct((rollouts, slot), jnp.float32)] + [
        jax.ShapeDtypeStruct((ROUTES.count(bit), slot), jnp.float32) for bit in BITS
    ]


def weight_specs(flips, blocks, widths):
    def row(step, part_ref, *rest):
        flip = flips[0]
        for f in range(1, len(flips)):
            flip = jnp.where(step < f * blocks, flip, flips[f])
        return (part_ref[0] ^ flip) * blocks + lax.rem(step, blocks)

    return [pl.BlockSpec((1, DEPTH), lambda k, *p: (0, row(k, *p)))] + [
        pl.BlockSpec((DEPTH, width), lambda k, *p: (row(k, *p), 0)) for width in widths
    ]


def x_spec(rows, blocks, f):
    return pl.BlockSpec((rows, DEPTH), lambda k, *p: (0, jnp.clip(k - f * blocks, 0, blocks - 1)))


def fixed(*shape):
    return pl.BlockSpec(shape, lambda k, *p: (0, 0))


def cost(rows, depth, columns):
    return pl.CostEstimate(
        flops=2 * rows * depth * columns,
        bytes_accessed=2 * depth * (rows + columns) + 4 * rows * columns,
        transcendentals=0,
    )


def sums_call(shared, flips, xs, head, begun=None):
    part, gain, weights = shared
    widths = [w.shape[1] for w in weights]
    groups = len(xs[0])
    blocks = xs[0][0].shape[1] // DEPTH
    counts = [x.shape[0] for x in xs[0]]
    outs = [(count, width) for count in counts for width in (widths[0], sum(widths[1:]), HD, HD)]
    given = [a for group in begun for a in group] if begun else []
    sums = pl.pallas_call(
        functools.partial(sums_kernel, len(flips), groups, begun is not None),
        grid_spec=pltpu.PrefetchScalarGridSpec(
            num_scalar_prefetch=1,
            grid=(len(flips) * blocks,),
            in_specs=[x_spec(count, blocks, f) for f in range(len(flips)) for count in counts]
            + weight_specs(flips, blocks, widths)
            + [pl.BlockSpec((1, DEPTH), lambda k, *p: (0, jnp.minimum(k, blocks - 1)))]
            + [fixed(*a.shape) for a in given],
            out_specs=[fixed(*shape) for shape in outs],
            scratch_shapes=[pltpu.VMEM((DEPTH, 2 * HD), jnp.bfloat16)],
        ),
        out_shape=[jax.ShapeDtypeStruct(shape, jnp.float32) for shape in outs],
        compiler_params=pltpu.CompilerParams(vmem_limit_bytes=24 << 20),
        cost_estimate=cost(sum(counts), len(flips) * blocks * DEPTH, sum(widths)),
        name="sums",
    )(part, *[x for row in xs for x in row], gain, *weights, head, *given)
    return [sums[4 * g : 4 * g + 4] for g in range(groups)]


def attend_call(shared, tables, begin, places, flips, xs, sums, before, last=None):
    part, gain, weights = shared
    widths = [w.shape[1] for w in weights]
    count, blocks = xs[0].shape[0], xs[0].shape[1] // DEPTH
    slot = tables[0].shape[0]
    tile = max(t for t in range(GRAIN, 97, GRAIN) if count % t == 0)
    stacked = widths[0] // HD * tile
    scalars, given, lines, space = [part, places], [], [], []
    if last:
        info, ahead, rollouts, rows = last
        scalars, given, lines = [*scalars, info], [ahead], line_shapes(rollouts, slot)
        space = [pltpu.VMEM((rows + 2 * HD, HD), jnp.float32)]
    outs = [
        jax.ShapeDtypeStruct((count, HD), jnp.float32),
        jax.ShapeDtypeStruct((slot, HD), jnp.bfloat16),
        jax.ShapeDtypeStruct((slot, HD), jnp.bfloat16),
    ]

    def kernel(*refs):
        n = len(scalars) + len(flips) + 4 + len(sums) + len(tables) + len(before)
        inputs, more, refs = refs[:n], refs[n : n + len(given)], refs[n + len(given) :]
        own, rest = refs[: len(outs)], refs[len(outs) :]
        extra, scratch = rest[: len(lines)], rest[len(lines) :]
        scratch, room = scratch[: len(scratch) - len(space)], scratch[len(scratch) - len(space) :]
        attend_kernel(
            slot, tile, begin, len(flips), last is not None,
            *inputs, *own, *scratch, *more, *extra, *room,
        )

    return pl.pallas_call(
        kernel,
        grid_spec=pltpu.PrefetchScalarGridSpec(
            num_scalar_prefetch=len(scalars),
            grid=(len(flips) * blocks,),
            in_specs=[x_spec(count, blocks, f) for f in range(len(flips))]
            + weight_specs(flips, blocks, widths)
            + [fixed(*a.shape) for a in (*sums, *tables, *before, *given)],
            out_specs=[fixed(*a.shape) for a in (*outs, *lines)],
            scratch_shapes=[
                pltpu.VMEM((count, widths[0]), jnp.float32),
                pltpu.VMEM((count, widths[1] + widths[2]), jnp.float32),
                pltpu.VMEM((count, HD), jnp.float32),
                pltpu.VMEM((count, HD), jnp.float32),
                pltpu.VMEM((count, HD), jnp.float32),
                pltpu.VMEM((count, HD), jnp.int32),
                pltpu.VMEM((slot + count, HD), jnp.bfloat16),
                pltpu.VMEM((slot + count, 2 * HD), jnp.bfloat16),
                pltpu.VMEM((stacked, HD), jnp.bfloat16),
                pltpu.VMEM((stacked, slot + tile), jnp.bfloat16),
                pltpu.VMEM((DEPTH, 2 * HD), jnp.bfloat16),
            ]
            + space,
        ),
        out_shape=outs + lines,
        compiler_params=pltpu.CompilerParams(vmem_limit_bytes=24 << 20),
        cost_estimate=cost(count, len(flips) * blocks * DEPTH, sum(widths)),
        name="attend",
    )(*scalars, *xs, gain, *weights, *sums, *tables, *before, *given)


def local(
    hidden,
    rewards,
    lengths,
    dest_shard,
    source_owner,
    pack_offset,
    segment_ids,
    norm_gain,
    w_query,
    w_key,
    w_value,
    value_head,
    folded_head,
):
    rollouts, slot = rewards.shape
    rows, part_width = hidden.shape
    q_width = w_query.shape[1]
    part = lax.axis_index("mp").astype(jnp.int32)[None]
    gain = norm_gain[None, :]
    weights = (w_query, w_key, w_value)

    positions = jnp.arange(slot, dtype=jnp.float32)
    half = HD // 2
    frequency = ROPE_BASE ** (-jnp.arange(half, dtype=jnp.float32) / half)
    angles = positions[:, None] * frequency[None, :]
    cosine = jnp.concatenate([jnp.cos(angles)] * 2, axis=1)
    sine = jnp.concatenate([-jnp.sin(angles), jnp.sin(angles)], axis=1)

    slot_blocks = slot // GRAIN
    packed = segment_ids.shape[0]
    first = packed * 7 // 8
    second = packed // 2
    extra = packed // 8
    rest = rows - first - second
    whole = jax.ShapeDtypeStruct
    anywhere = pl.BlockSpec(memory_space=pl.ANY)
    scalars = pl.BlockSpec(memory_space=pltpu.SMEM)
    onchip = pl.BlockSpec(memory_space=pltpu.VMEM)
    blocks_in_all = rows // GRAIN
    shared = (part, gain, weights)
    head = value_head[None, :]
    tables = (cosine, sine, folded_head.reshape(q_width // HD, HD))
    vmem = pltpu.CompilerParams(vmem_limit_bytes=12 << 20)

    places_first, x_first = pl.pallas_call(
        functools.partial(first_pack_kernel, slot_blocks),
        in_specs=[scalars, anywhere],
        out_specs=[scalars, onchip],
        out_shape=[whole((first // GRAIN,), jnp.int32), whole((first, part_width), hidden.dtype)],
        scratch_shapes=[pltpu.SemaphoreType.DMA],
        compiler_params=vmem,
        name="first_pack",
    )(lengths, hidden)
    far_first = swapped(x_first, "mp", 2)
    near_first = swapped(x_first, "mp", 1)

    owners = lax.axis_size("dp")
    me = lax.axis_index("dp").astype(jnp.int32)
    everyone = lax.psum(
        jnp.where(jnp.arange(owners)[:, None] == me, lengths[None, :], 0), "dp"
    ).reshape(-1)
    source, places, info, *ships = pl.pallas_call(
        functools.partial(
            plan_kernel, slot_blocks, first // GRAIN, (first + second) // GRAIN, extra // GRAIN
        ),
        in_specs=[scalars, scalars, anywhere],
        out_specs=[scalars, scalars, scalars] + [onchip] * len(BITS),
        out_shape=[
            whole((blocks_in_all,), jnp.int32),
            whole((blocks_in_all,), jnp.int32),
            whole((64,), jnp.int32),
        ]
        + [whole((ROUTES.count(bit) * slot, part_width), hidden.dtype) for bit in BITS],
        scratch_shapes=[pltpu.SMEM((owners,), jnp.int32)] * 4
        + [pltpu.SemaphoreType.DMA((len(ROUTES),))],
        compiler_params=vmem,
        name="plan",
    )(me[None], everyone, hidden)
    arrivals = [swapped(ship, "dp", bit) for ship, bit in zip(ships, BITS, strict=True)]

    shipped = info[SHIPPED : SHIPPED + len(ROUTES)] > 0
    ship_slots = info[SHIP_SLOT : SHIP_SLOT + len(ROUTES)]
    mine = shipped[:, None] & (ship_slots[:, None] == jnp.arange(rollouts)[None, :])

    def pack(begin, count):
        return pl.pallas_call(
            functools.partial(pack_kernel, begin, slot_blocks),
            in_specs=[scalars, anywhere] + [anywhere] * len(BITS),
            out_specs=onchip,
            out_shape=whole((count, part_width), hidden.dtype),
            scratch_shapes=[pltpu.SemaphoreType.DMA],
            compiler_params=vmem,
            name="pack",
        )(source, hidden, *arrivals)

    def attend(begin, places, far, sums, before):
        return attend_call(
            shared, tables, begin, places, (2, 3), [far, swapped(far, "mp", 1)], sums, before
        )

    nothing = jnp.zeros((slot, HD), jnp.bfloat16)
    before = (nothing, nothing)
    (sums_first,) = sums_call(shared, (0, 1), [[x_first], [near_first]], head)
    mine, over, sums_first, *arrivals = lax.optimization_barrier(
        (mine, info[OVERFLOW], sums_first, *arrivals)
    )
    x_second = pack(first, second)
    far_first, x_second = lax.optimization_barrier((far_first, x_second))
    far_second = swapped(x_second, "mp", 2)
    near_second = swapped(x_second, "mp", 1)
    total_first, *before = attend(0, places_first, far_first, sums_first, before)
    x_second, near_second, _ = lax.optimization_barrier((x_second, near_second, total_first))
    (sums_second,) = sums_call(shared, (0, 1), [[x_second], [near_second]], head)
    far_second, sums_second = lax.optimization_barrier((far_second, sums_second))
    far_near = swapped(far_second, "mp", 1)
    (sums_second,) = sums_call(shared, (2,), [[far_second]], head, begun=[sums_second])
    far_near, sums_second = lax.optimization_barrier((far_near, sums_second))
    total_second, key_rows, val_rows, *lines = attend_call(
        shared, tables, first, places, (3,), [far_near], sums_second, before,
        last=(info, total_first, rollouts, rows),
    )

    def overflow(count, _):
        begin = first + second
        x = pack(begin, count)
        (sums,) = sums_call(shared, (0, 1), [[x], [swapped(x, "mp", 1)]], head)
        far = swapped(x, "mp", 2)
        total_rest, *_ = attend(begin, places, far, sums, (key_rows, val_rows))
        return tuple(pl.pallas_call(
            functools.partial(unpack_kernel, slot),
            in_specs=[scalars] + [onchip] * 3,
            out_shape=line_shapes(rollouts, slot),
            scratch_shapes=[pltpu.VMEM((rows + 2 * HD, HD), jnp.float32)],
            name="unpack",
        )(info, total_first, total_second, total_rest))

    more = [functools.partial(overflow, count) for count in (extra, rest)]
    slot_terms, *backs = lax.switch(over, [tuple, *more], lines)
    backs = [swapped(back, "dp", bit) for back, bit in zip(backs, BITS, strict=True)]
    for r, bit in enumerate(ROUTES):
        back = backs[BITS.index(bit)][ROUTES[:r].count(bit)]
        slot_terms = jnp.where(mine[r, :, None], back[None, :], slot_terms)
    slot_values = slot_terms
    for bit in (1, 2):
        slot_values = slot_values + swapped(slot_values, "mp", bit)

    step_ids = jnp.arange(slot, dtype=jnp.int32)
    live_mask = step_ids[None, :] < lengths[:, None]
    values = jnp.where(live_mask, slot_values, 0.0)
    next_live = step_ids[None, :] + 1 < lengths[:, None]
    following = jnp.concatenate([values[:, 1:], jnp.zeros((rollouts, 1), jnp.float32)], axis=1)
    one_step = jnp.where(
        live_mask, rewards + DISCOUNT * jnp.where(next_live, following, 0.0) - values, 0.0
    )
    lag_matrix = (step_ids[:, None] - step_ids[None, :]).astype(jnp.float32)
    decay_table = jnp.where(
        lag_matrix >= 0, jnp.exp(lag_matrix * math.log(DISCOUNT * SMOOTHING)), 0.0
    )
    advantages = jnp.dot(one_step, decay_table, precision=lax.Precision.HIGHEST)
    return (values, advantages)


def solution(mesh):
    return jax.shard_map(
        local,
        mesh=mesh,
        in_specs=(
            P("dp", "mp"),
            P("dp", None),
            P("dp"),
            P("dp"),
            P("dp"),
            P("dp"),
            P("dp"),
            P(),
            P(None, "mp"),
            P(None, "mp"),
            P(None, "mp"),
            P("mp"),
            P("mp"),
        ),
        out_specs=(P("dp", None), P("dp", None)),
        check_vma=False,
    )
```

```python
import functools
import math

import jax
import jax.numpy as jnp
from jax import lax
from jax.experimental import pallas as pl
from jax.experimental.pallas import tpu as pltpu
from jax.sharding import PartitionSpec as P

HD = 128
EPSILON = 1e-05
DISCOUNT = 0.99
SMOOTHING = 0.95
ROPE_BASE = 500000.0
DEPTH = 1024
PARTS = 4
STAGED = (2, 3)
GRAIN = 16
ROUTES = (1, 2, 4, 1)
BITS = (1, 2, 4)
SLOT_AT, ARRIVED_AT, SHIP_SLOT, SHIPPED, OVERFLOW = 0, 16, 24, 32, 40


def swapped(value, axis, bit):
    length = lax.axis_size(axis)
    return lax.ppermute(value, axis, [(i, i ^ bit) for i in range(length)])


def lane_groups(value):
    total = value[:, :HD]
    for at in range(HD, value.shape[1], HD):
        total = total + value[:, at : at + HD]
    return total


def add_products(x, gain_ref, w_refs, q_acc, kv_acc, ss_acc, wkv):
    if len(w_refs) == 1:
        width = q_acc.shape[1]
        wq, w_rest = w_refs[0][:, :width], w_refs[0][:, width:]
    else:
        wkv[:, :HD] = w_refs[1][...]
        wkv[:, HD:] = w_refs[2][...]
        wq, w_rest = w_refs[0][...], wkv[...]
    xf = x.astype(jnp.float32)
    ss_acc[...] += lane_groups(xf * xf)
    scaled = (xf * gain_ref[...]).astype(jnp.bfloat16)
    q_acc[...] += jnp.dot(scaled, wq, preferred_element_type=jnp.float32)
    kv_acc[...] += jnp.dot(scaled, w_rest, preferred_element_type=jnp.float32)


def by_part(step, blocks, x_refs, act):
    for f, refs in enumerate(x_refs):

        @pl.when((step >= f * blocks) & (step < (f + 1) * blocks))
        def _(f=f, refs=refs):
            act(f, refs)


def sums_kernel(parts, arrays, groups, begun, part_ref, *refs):
    refs = list(refs)
    take = lambda n: [refs.pop(0) for _ in range(n)]
    x_refs = [take(groups) for _ in range(parts)]
    (gain_ref,) = take(1)
    weights = take(arrays)
    (head_ref,) = take(1)
    begun_refs = [take(4) for _ in range(groups)] if begun else None
    outs = [take(4) for _ in range(groups)]
    (wkv,) = take(1)
    step = pl.program_id(0)

    @pl.when(step == 0)
    def _():
        for g, out in enumerate(outs):
            for i, ref in enumerate(out):
                ref[...] = begun_refs[g][i][...] if begun else jnp.zeros_like(ref)

    def act(f, rows):
        for x_ref, (q_ref, kv_ref, ss_ref, vt_ref) in zip(rows, outs, strict=True):
            x = x_ref[...]
            if f == 0 and not begun:
                vt_ref[...] += lane_groups(x.astype(jnp.float32) * head_ref[...])
            add_products(x, gain_ref, weights, q_ref, kv_ref, ss_ref, wkv)

    by_part(step, pl.num_programs(0) // parts, x_refs, act)


def turned(value, cosine, sine):
    return (value * cosine + pltpu.roll(value, HD // 2, 1) * sine).astype(jnp.bfloat16)


def attend_kernel(slot, tile, begin, parts, arrays, last, part_ref, place_ref, *refs):
    if last:
        info_ref, refs = refs[0], refs[1:]
    x_refs, refs = [[ref] for ref in refs[:parts]], refs[parts:]
    gain_ref, weights, refs = refs[0], refs[1 : 1 + arrays], refs[1 + arrays :]
    if last:
        (total_ref, line_ref, *back_refs, rows_ref), refs = refs[-3 - len(BITS) :], refs[: -3 - len(BITS)]
    (
        q_ref, kv_ref, ss_ref, vt_ref, cos_ref, sin_ref, folded_ref, key_in, val_in,
        out_ref, key_out, val_out, q_acc, kv_acc, ss_acc, cos_rows, sin_rows, place_rows, keys, vals,
        queries, probs, wkv,
    ) = refs
    step = pl.program_id(0)
    steps = pl.num_programs(0)
    rows = q_acc.shape[0]
    heads = q_acc.shape[1] // HD

    @pl.when(step == 0)
    def _():
        q_acc[...] = q_ref[...]
        kv_acc[...] = kv_ref[...]
        ss_acc[...] = ss_ref[...]
        keys[:slot, :] = key_in[...]
        vals[:slot, :HD] = val_in[...]
        vals[:, HD:] = jnp.ones((slot + rows, HD), jnp.bfloat16)
        inner = lax.broadcasted_iota(jnp.int32, (GRAIN, HD), 0)

        def place(b, carry):
            at = place_ref[begin // GRAIN + b]
            here = pl.ds(pl.multiple_of(b * GRAIN, GRAIN), GRAIN)
            there = pl.ds(pl.multiple_of(at * GRAIN, GRAIN), GRAIN)
            cos_rows[here, :] = cos_ref[there, :]
            sin_rows[here, :] = sin_ref[there, :]
            place_rows[here, :] = inner + at * GRAIN
            return carry

        lax.fori_loop(0, rows // GRAIN, place, 0)

    def act(f, rows):
        add_products(rows[0][...], gain_ref, weights, q_acc, kv_acc, ss_acc, wkv)

    by_part(step, steps // parts, x_refs, act)

    @pl.when(step == steps - 1)
    def _():
        features = DEPTH * steps // parts * PARTS
        scale = lax.rsqrt(jnp.sum(ss_acc[...], axis=1, keepdims=True) / features + EPSILON)
        keys[slot:, :] = turned(kv_acc[:, :HD] * scale, cos_rows[...], sin_rows[...])
        vals[slot:, :HD] = (kv_acc[:, HD:] * scale).astype(jnp.bfloat16)
        key_out[...] = keys[rows:, :]
        val_out[...] = vals[rows:, :HD]
        back = (
            lax.broadcasted_iota(jnp.int32, (tile, slot + tile), 0)
            + slot
            - lax.broadcasted_iota(jnp.int32, (tile, slot + tile), 1)
        )

        def one_tile(t, carry):
            here = pl.ds(pl.multiple_of(t * tile, GRAIN), tile)
            window = pl.ds(pl.multiple_of(t * tile, GRAIN), slot + tile)
            mean = jnp.sum(ss_acc[here, :], axis=1, keepdims=True) / features
            scale = lax.rsqrt(mean + EPSILON) * (math.log2(math.e) / math.sqrt(HD))
            cosine, sine = cos_rows[here, :] * scale, sin_rows[here, :] * scale
            bias = jnp.where((back >= 0) & (back <= place_rows[here, :1]), 0.0, -1e30)
            for h in range(heads):
                turned_h = turned(q_acc[here, h * HD : (h + 1) * HD], cosine, sine)
                queries[h * tile : (h + 1) * tile, :] = turned_h
            scores = lax.dot_general(
                queries[...], keys[window, :], (((1,), (1,)), ((), ())),
                preferred_element_type=jnp.float32,
            )
            for h in range(heads):
                score = scores[h * tile : (h + 1) * tile, :] + bias
                exps = jnp.exp2(score - jnp.max(score, axis=1, keepdims=True))
                probs[h * tile : (h + 1) * tile, :] = exps.astype(jnp.bfloat16)
            attended = jnp.dot(probs[...], vals[window, :], preferred_element_type=jnp.float32)
            total = vt_ref[here, :]
            for h in range(heads):
                mine = attended[h * tile : (h + 1) * tile, :]
                total = total + mine[:, :HD] / mine[:, HD:] * folded_ref[h : h + 1, :]
            out_ref[here, :] = total
            return carry

        lax.fori_loop(0, rows // tile, one_tile, 0, unroll=2)
        if last:
            rows_ref[:begin, :] = total_ref[...]
            rows_ref[begin : begin + rows, :] = out_ref[...]
            unpack(slot, info_ref, rows_ref, line_ref, back_refs)


def start_copy(source, source_block, target, target_block, sem):
    pltpu.make_async_copy(
        source.at[pl.ds(pl.multiple_of(source_block * GRAIN, GRAIN), GRAIN)],
        target.at[pl.ds(pl.multiple_of(target_block * GRAIN, GRAIN), GRAIN)],
        sem,
    ).start()


def wait_copies(source, target, sem):
    pltpu.make_async_copy(source.at[pl.ds(0, target.shape[0])], target, sem).wait()


def blocks_of(length):
    return (length + (GRAIN - 1)) >> (GRAIN.bit_length() - 1)


def lay_out(begin, count, slot_blocks, first_block, source_ref, place_ref):
    def enter(j, carry):
        source_ref[begin + j] = first_block + j
        place_ref[begin + j] = j
        return carry

    lax.fori_loop(0, count, enter, 0)


def lay_out_fill(slot_blocks, source_ref, place_ref):
    def enter(b, carry):
        source_ref[b] = b
        place_ref[b] = lax.rem(b, slot_blocks)
        return carry

    lax.fori_loop(0, source_ref.shape[0], enter, 0)


def first_pack_kernel(slot_blocks, lengths_ref, hidden_ref, place_ref, out_ref, sem):
    total = out_ref.shape[0] // GRAIN

    def copy(j, carry, at, first_block):
        start_copy(hidden_ref, first_block + j, out_ref, at + j, sem)
        place_ref[at + j] = j
        return carry

    at = jnp.int32(0)
    for i in range(lengths_ref.shape[0]):
        count = jnp.minimum(blocks_of(lengths_ref[i]), total - at)
        lax.fori_loop(0, count, functools.partial(copy, at=at, first_block=i * slot_blocks), 0)
        at = at + count

    def fill(b, carry):
        start_copy(hidden_ref, 0, out_ref, b, sem)
        place_ref[b] = 0
        return carry

    lax.fori_loop(at, total, fill, 0)
    wait_copies(hidden_ref, out_ref, sem)


def plan_kernel(
    slot_blocks, first_blocks, capacity, extra, me_ref, lengths_ref, hidden_ref,
    source_ref, place_ref, info_ref, *refs,
):
    kept, load, sent, moved, sems = refs[len(BITS) :]
    size = slot_blocks * GRAIN
    ships = [
        refs[BITS.index(bit)].at[pl.ds(ROUTES[:r].count(bit) * size, size)]
        for r, bit in enumerate(ROUTES)
    ]
    me = me_ref[0]
    owners = kept.shape[0]
    rollouts = lengths_ref.shape[0] // owners

    def begin(o, carry):
        total = jnp.int32(0)
        for i in range(rollouts):
            total = total + blocks_of(lengths_ref[o * rollouts + i])
        kept[o] = total
        load[o] = jnp.maximum(total, first_blocks)
        sent[o] = 0
        return carry

    lax.fori_loop(0, owners, begin, 0)
    arrived = []
    for r, bit in enumerate(ROUTES):

        def choose(o, carry):
            count = blocks_of(lengths_ref[o * rollouts + rollouts - 1 - sent[o]])
            useful = (kept[o] - count >= first_blocks) & (load[o ^ bit] + count < load[o])
            moved[o] = jnp.where(useful, count, 0)
            return carry

        lax.fori_loop(0, owners, choose, 0)
        slot_now = rollouts - 1 - sent[me]
        info_ref[SHIP_SLOT + r] = slot_now
        info_ref[SHIPPED + r] = jnp.where(moved[me] > 0, 1, 0)
        arrived.append(moved[me ^ bit])
        pltpu.make_async_copy(
            hidden_ref.at[pl.ds(pl.multiple_of(slot_now * size, GRAIN), size)],
            ships[r],
            sems.at[r],
        ).start()

        def move(o, carry):
            kept[o] = kept[o] - moved[o]
            load[o] = load[o] - moved[o] + moved[o ^ bit]
            sent[o] = sent[o] + jnp.where(moved[o] > 0, 1, 0)
            return carry

        lax.fori_loop(0, owners, move, 0)

    most = lax.fori_loop(0, owners, lambda o, m: jnp.maximum(m, load[o]), jnp.int32(0))
    more = jnp.where(most > capacity + extra, 2, 1)
    info_ref[OVERFLOW] = jnp.where(most > capacity, more, 0)

    lay_out_fill(slot_blocks, source_ref, place_ref)
    at = jnp.int32(0)
    for i in range(rollouts):
        here = i < rollouts - sent[me]
        count = jnp.where(here, blocks_of(lengths_ref[me * rollouts + i]), 0)
        info_ref[SLOT_AT + i] = jnp.where(here, at, 0)
        lay_out(at, count, slot_blocks, i * slot_blocks, source_ref, place_ref)
        at = at + count
    at = jnp.maximum(at, first_blocks)
    for r in range(len(ROUTES)):
        info_ref[ARRIVED_AT + r] = jnp.where(arrived[r] > 0, at, 0)
        lay_out(at, arrived[r], slot_blocks, (rollouts + r) * slot_blocks, source_ref, place_ref)
        at = at + arrived[r]
    for r in range(len(ROUTES)):
        pltpu.make_async_copy(hidden_ref.at[pl.ds(0, size)], ships[r], sems.at[r]).wait()


def pack_kernel(begin, slot_blocks, source_ref, hidden_ref, *refs):
    out_ref, sem = refs[len(BITS) :]
    size = slot_blocks * GRAIN
    arrivals = [
        refs[BITS.index(bit)].at[pl.ds(ROUTES[:r].count(bit) * size, size)]
        for r, bit in enumerate(ROUTES)
    ]
    own = hidden_ref.shape[0] // GRAIN

    def start(b, carry):
        block = source_ref[begin // GRAIN + b]

        @pl.when(block < own)
        def _():
            start_copy(hidden_ref, block, out_ref, b, sem)

        for r, arrival in enumerate(arrivals):
            low = own + r * slot_blocks

            @pl.when((block >= low) & (block < low + slot_blocks))
            def _(arrival=arrival, low=low):
                start_copy(arrival, block - low, out_ref, b, sem)

        return carry

    lax.fori_loop(0, out_ref.shape[0] // GRAIN, start, 0)
    wait_copies(hidden_ref, out_ref, sem)


def unpack(slot, info_ref, rows_ref, out_ref, back_refs):
    rollouts = out_ref.shape[0]

    def line(block):
        part = rows_ref[pl.ds(pl.multiple_of(block * GRAIN, GRAIN), 2 * HD), :]
        return jnp.sum(part.T, axis=0, keepdims=True)[:, :slot]

    for i in range(rollouts):
        out_ref[i : i + 1, :] = line(info_ref[SLOT_AT + i])
    for r, bit in enumerate(ROUTES):
        back_ref, i = back_refs[BITS.index(bit)], ROUTES[:r].count(bit)
        back_ref[i : i + 1, :] = line(info_ref[ARRIVED_AT + r])


def unpack_kernel(slot, info_ref, *refs):
    totals, out_ref, back_refs, rows_ref = refs[:3], refs[3], refs[4:-1], refs[-1]
    at = 0
    for total in totals:
        rows_ref[at : at + total.shape[0], :] = total[...]
        at += total.shape[0]
    rows_ref[at:, :] = jnp.zeros((rows_ref.shape[0] - at, HD), jnp.float32)
    unpack(slot, info_ref, rows_ref, out_ref, back_refs)


def line_shapes(rollouts, slot):
    return [jax.ShapeDtypeStruct((rollouts, slot), jnp.float32)] + [
        jax.ShapeDtypeStruct((ROUTES.count(bit), slot), jnp.float32) for bit in BITS
    ]


def weight_specs(flips, blocks, widths):
    def row(step, part_ref, *rest):
        flip = flips[0]
        for f in range(1, len(flips)):
            flip = jnp.where(step < f * blocks, flip, flips[f])
        return (part_ref[0] ^ flip) * blocks + lax.rem(step, blocks)

    def staged_row(step, *rest):
        return (flips[0] - STAGED[0]) * blocks + step

    held = row if len(widths) > 1 else staged_row
    return [pl.BlockSpec((1, DEPTH), lambda k, *p: (0, row(k, *p)))] + [
        pl.BlockSpec((DEPTH, width), lambda k, *p: (held(k, *p), 0)) for width in widths
    ]


def stage_kernel(part_ref, *refs):
    weights, (out_ref, sems) = refs[:-2], refs[-2:]
    height = out_ref.shape[0] // len(STAGED)
    copies = []
    for f, flip in enumerate(STAGED):
        at = 0
        for i, w_ref in enumerate(weights):
            width = w_ref.shape[1]
            begin = pl.multiple_of((part_ref[0] ^ flip) * height, height)
            copies.append(
                pltpu.make_async_copy(
                    w_ref.at[pl.ds(begin, height)],
                    out_ref.at[pl.ds(f * height, height), pl.ds(at, width)],
                    sems.at[f * len(weights) + i],
                )
            )
            at += width
    for copy in copies:
        copy.start()
    for copy in copies:
        copy.wait()


def x_spec(rows, blocks, f):
    return pl.BlockSpec((rows, DEPTH), lambda k, *p: (0, jnp.clip(k - f * blocks, 0, blocks - 1)))


def fixed(*shape):
    return pl.BlockSpec(shape, lambda k, *p: (0, 0))


def cost(rows, depth, columns):
    return pl.CostEstimate(
        flops=2 * rows * depth * columns,
        bytes_accessed=2 * depth * (rows + columns) + 4 * rows * columns,
        transcendentals=0,
    )


def sums_call(shared, flips, xs, head, begun=None):
    part, gain, weights = shared
    widths = [w.shape[1] for w in weights]
    groups = len(xs[0])
    blocks = xs[0][0].shape[1] // DEPTH
    counts = [x.shape[0] for x in xs[0]]
    columns = sum(widths)
    outs = [(count, width) for count in counts for width in (columns - 2 * HD, 2 * HD, HD, HD)]
    given = [a for group in begun for a in group] if begun else []
    sums = pl.pallas_call(
        functools.partial(sums_kernel, len(flips), len(weights), groups, begun is not None),
        grid_spec=pltpu.PrefetchScalarGridSpec(
            num_scalar_prefetch=1,
            grid=(len(flips) * blocks,),
            in_specs=[x_spec(count, blocks, f) for f in range(len(flips)) for count in counts]
            + weight_specs(flips, blocks, widths)
            + [pl.BlockSpec((1, DEPTH), lambda k, *p: (0, jnp.minimum(k, blocks - 1)))]
            + [fixed(*a.shape) for a in given],
            out_specs=[fixed(*shape) for shape in outs],
            scratch_shapes=[pltpu.VMEM((DEPTH, 2 * HD), jnp.bfloat16)],
        ),
        out_shape=[jax.ShapeDtypeStruct(shape, jnp.float32) for shape in outs],
        compiler_params=pltpu.CompilerParams(vmem_limit_bytes=24 << 20),
        cost_estimate=cost(sum(counts), len(flips) * blocks * DEPTH, sum(widths)),
        name="sums",
    )(part, *[x for row in xs for x in row], gain, *weights, head, *given)
    return [sums[4 * g : 4 * g + 4] for g in range(groups)]


def attend_call(shared, tables, begin, places, flips, xs, sums, before, last=None):
    part, gain, weights = shared
    widths = [w.shape[1] for w in weights]
    count, blocks = xs[0].shape[0], xs[0].shape[1] // DEPTH
    slot = tables[0].shape[0]
    tile = max(t for t in range(GRAIN, 97, GRAIN) if count % t == 0)
    q_width = sum(widths) - 2 * HD
    stacked = q_width // HD * tile
    scalars, given, lines, space = [part, places], [], [], []
    if last:
        info, ahead, rollouts, rows = last
        scalars, given, lines = [*scalars, info], [ahead], line_shapes(rollouts, slot)
        space = [pltpu.VMEM((rows + 2 * HD, HD), jnp.float32)]
    outs = [
        jax.ShapeDtypeStruct((count, HD), jnp.float32),
        jax.ShapeDtypeStruct((slot, HD), jnp.bfloat16),
        jax.ShapeDtypeStruct((slot, HD), jnp.bfloat16),
    ]

    def kernel(*refs):
        n = len(scalars) + len(flips) + 1 + len(weights) + len(sums) + len(tables) + len(before)
        inputs, more, refs = refs[:n], refs[n : n + len(given)], refs[n + len(given) :]
        own, rest = refs[: len(outs)], refs[len(outs) :]
        extra, scratch = rest[: len(lines)], rest[len(lines) :]
        scratch, room = scratch[: len(scratch) - len(space)], scratch[len(scratch) - len(space) :]
        attend_kernel(
            slot, tile, begin, len(flips), len(weights), last is not None,
            *inputs, *own, *scratch, *more, *extra, *room,
        )

    return pl.pallas_call(
        kernel,
        grid_spec=pltpu.PrefetchScalarGridSpec(
            num_scalar_prefetch=len(scalars),
            grid=(len(flips) * blocks,),
            in_specs=[x_spec(count, blocks, f) for f in range(len(flips))]
            + weight_specs(flips, blocks, widths)
            + [fixed(*a.shape) for a in (*sums, *tables, *before, *given)],
            out_specs=[fixed(*a.shape) for a in (*outs, *lines)],
            scratch_shapes=[
                pltpu.VMEM((count, q_width), jnp.float32),
                pltpu.VMEM((count, 2 * HD), jnp.float32),
                pltpu.VMEM((count, HD), jnp.float32),
                pltpu.VMEM((count, HD), jnp.float32),
                pltpu.VMEM((count, HD), jnp.float32),
                pltpu.VMEM((count, HD), jnp.int32),
                pltpu.VMEM((slot + count, HD), jnp.bfloat16),
                pltpu.VMEM((slot + count, 2 * HD), jnp.bfloat16),
                pltpu.VMEM((stacked, HD), jnp.bfloat16),
                pltpu.VMEM((stacked, slot + tile), jnp.bfloat16),
                pltpu.VMEM((DEPTH, 2 * HD), jnp.bfloat16),
            ]
            + space,
        ),
        out_shape=outs + lines,
        compiler_params=pltpu.CompilerParams(vmem_limit_bytes=24 << 20),
        cost_estimate=cost(count, len(flips) * blocks * DEPTH, sum(widths)),
        name="attend",
    )(*scalars, *xs, gain, *weights, *sums, *tables, *before, *given)


def local(
    hidden,
    rewards,
    lengths,
    dest_shard,
    source_owner,
    pack_offset,
    segment_ids,
    norm_gain,
    w_query,
    w_key,
    w_value,
    value_head,
    folded_head,
):
    rollouts, slot = rewards.shape
    rows, part_width = hidden.shape
    q_width = w_query.shape[1]
    part = lax.axis_index("mp").astype(jnp.int32)[None]
    gain = norm_gain[None, :]
    weights = (w_query, w_key, w_value)

    positions = jnp.arange(slot, dtype=jnp.float32)
    half = HD // 2
    frequency = ROPE_BASE ** (-jnp.arange(half, dtype=jnp.float32) / half)
    angles = positions[:, None] * frequency[None, :]
    cosine = jnp.concatenate([jnp.cos(angles)] * 2, axis=1)
    sine = jnp.concatenate([-jnp.sin(angles), jnp.sin(angles)], axis=1)

    slot_blocks = slot // GRAIN
    packed = segment_ids.shape[0]
    first = packed * 7 // 8
    second = packed // 2
    extra = packed // 8
    rest = rows - first - second
    whole = jax.ShapeDtypeStruct
    anywhere = pl.BlockSpec(memory_space=pl.ANY)
    scalars = pl.BlockSpec(memory_space=pltpu.SMEM)
    onchip = pl.BlockSpec(memory_space=pltpu.VMEM)
    blocks_in_all = rows // GRAIN
    shared = (part, gain, weights)
    head = value_head[None, :]
    tables = (cosine, sine, folded_head.reshape(q_width // HD, HD))
    vmem = pltpu.CompilerParams(vmem_limit_bytes=12 << 20)

    places_first, x_first = pl.pallas_call(
        functools.partial(first_pack_kernel, slot_blocks),
        in_specs=[scalars, anywhere],
        out_specs=[scalars, onchip],
        out_shape=[whole((first // GRAIN,), jnp.int32), whole((first, part_width), hidden.dtype)],
        scratch_shapes=[pltpu.SemaphoreType.DMA],
        compiler_params=vmem,
        name="first_pack",
    )(lengths, hidden)
    far_first = swapped(x_first, "mp", 2)
    near_first = swapped(x_first, "mp", 1)

    owners = lax.axis_size("dp")
    me = lax.axis_index("dp").astype(jnp.int32)
    everyone = lax.psum(
        jnp.where(jnp.arange(owners)[:, None] == me, lengths[None, :], 0), "dp"
    ).reshape(-1)
    source, places, info, *ships = pl.pallas_call(
        functools.partial(
            plan_kernel, slot_blocks, first // GRAIN, (first + second) // GRAIN, extra // GRAIN
        ),
        in_specs=[scalars, scalars, anywhere],
        out_specs=[scalars, scalars, scalars] + [onchip] * len(BITS),
        out_shape=[
            whole((blocks_in_all,), jnp.int32),
            whole((blocks_in_all,), jnp.int32),
            whole((64,), jnp.int32),
        ]
        + [whole((ROUTES.count(bit) * slot, part_width), hidden.dtype) for bit in BITS],
        scratch_shapes=[pltpu.SMEM((owners,), jnp.int32)] * 4
        + [pltpu.SemaphoreType.DMA((len(ROUTES),))],
        compiler_params=vmem,
        name="plan",
    )(me[None], everyone, hidden)
    arrivals = [swapped(ship, "dp", bit) for ship, bit in zip(ships, BITS, strict=True)]

    shipped = info[SHIPPED : SHIPPED + len(ROUTES)] > 0
    ship_slots = info[SHIP_SLOT : SHIP_SLOT + len(ROUTES)]
    mine = shipped[:, None] & (ship_slots[:, None] == jnp.arange(rollouts)[None, :])

    def pack(begin, count):
        return pl.pallas_call(
            functools.partial(pack_kernel, begin, slot_blocks),
            in_specs=[scalars, anywhere] + [anywhere] * len(BITS),
            out_specs=onchip,
            out_shape=whole((count, part_width), hidden.dtype),
            scratch_shapes=[pltpu.SemaphoreType.DMA],
            compiler_params=vmem,
            name="pack",
        )(source, hidden, *arrivals)

    def attend(begin, places, far, sums, before):
        return attend_call(
            shared, tables, begin, places, (2, 3), [far, swapped(far, "mp", 1)], sums, before
        )

    nothing = jnp.zeros((slot, HD), jnp.bfloat16)
    before = (nothing, nothing)
    (sums_first,) = sums_call(shared, (0, 1), [[x_first], [near_first]], head)
    mine, over, sums_first, *arrivals = lax.optimization_barrier(
        (mine, info[OVERFLOW], sums_first, *arrivals)
    )
    x_second = pack(first, second)
    far_first, x_second = lax.optimization_barrier((far_first, x_second))
    far_second = swapped(x_second, "mp", 2)
    near_second = swapped(x_second, "mp", 1)
    total_first, *before = attend(0, places_first, far_first, sums_first, before)
    x_second, near_second, _ = lax.optimization_barrier((x_second, near_second, total_first))
    (sums_second,) = sums_call(shared, (0, 1), [[x_second], [near_second]], head)
    part_then, sums_second = lax.optimization_barrier((part, sums_second))
    staged = pl.pallas_call(
        stage_kernel,
        in_specs=[scalars] + [anywhere] * len(weights),
        out_specs=onchip,
        out_shape=whole(
            (len(STAGED) * part_width, sum(w.shape[1] for w in weights)), w_query.dtype
        ),
        scratch_shapes=[pltpu.SemaphoreType.DMA((len(STAGED) * len(weights),))],
        compiler_params=pltpu.CompilerParams(vmem_limit_bytes=24 << 20),
        name="stage",
    )(part_then, *weights)
    far_second, sums_second, staged = lax.optimization_barrier((far_second, sums_second, staged))
    held = (part, gain, (staged,))
    far_near = swapped(far_second, "mp", 1)
    (sums_second,) = sums_call(held, (2,), [[far_second]], head, begun=[sums_second])
    far_near, sums_second = lax.optimization_barrier((far_near, sums_second))
    total_second, key_rows, val_rows, *lines = attend_call(
        held, tables, first, places, (3,), [far_near], sums_second, before,
        last=(info, total_first, rollouts, rows),
    )

    def overflow(count, _):
        begin = first + second
        x = pack(begin, count)
        (sums,) = sums_call(shared, (0, 1), [[x], [swapped(x, "mp", 1)]], head)
        far = swapped(x, "mp", 2)
        total_rest, *_ = attend(begin, places, far, sums, (key_rows, val_rows))
        return tuple(pl.pallas_call(
            functools.partial(unpack_kernel, slot),
            in_specs=[scalars] + [onchip] * 3,
            out_shape=line_shapes(rollouts, slot),
            scratch_shapes=[pltpu.VMEM((rows + 2 * HD, HD), jnp.float32)],
            name="unpack",
        )(info, total_first, total_second, total_rest))

    more = [functools.partial(overflow, count) for count in (extra, rest)]
    slot_terms, *backs = lax.switch(over, [tuple, *more], lines)
    backs = [swapped(back, "dp", bit) for back, bit in zip(backs, BITS, strict=True)]
    for r, bit in enumerate(ROUTES):
        back = backs[BITS.index(bit)][ROUTES[:r].count(bit)]
        slot_terms = jnp.where(mine[r, :, None], back[None, :], slot_terms)
    slot_values = slot_terms
    for bit in (1, 2):
        slot_values = slot_values + swapped(slot_values, "mp", bit)

    step_ids = jnp.arange(slot, dtype=jnp.int32)
    live_mask = step_ids[None, :] < lengths[:, None]
    values = jnp.where(live_mask, slot_values, 0.0)
    next_live = step_ids[None, :] + 1 < lengths[:, None]
    following = jnp.concatenate([values[:, 1:], jnp.zeros((rollouts, 1), jnp.float32)], axis=1)
    one_step = jnp.where(
        live_mask, rewards + DISCOUNT * jnp.where(next_live, following, 0.0) - values, 0.0
    )
    lag_matrix = (step_ids[:, None] - step_ids[None, :]).astype(jnp.float32)
    decay_table = jnp.where(
        lag_matrix >= 0, jnp.exp(lag_matrix * math.log(DISCOUNT * SMOOTHING)), 0.0
    )
    advantages = jnp.dot(one_step, decay_table, precision=lax.Precision.HIGHEST)
    return (values, advantages)


def solution(mesh):
    return jax.shard_map(
        local,
        mesh=mesh,
        in_specs=(
            P("dp", "mp"),
            P("dp", None),
            P("dp"),
            P("dp"),
            P("dp"),
            P("dp"),
            P("dp"),
            P(),
            P(None, "mp"),
            P(None, "mp"),
            P(None, "mp"),
            P("mp"),
            P("mp"),
        ),
        out_specs=(P("dp", None), P("dp", None)),
        check_vma=False,
    )
```
